256 devices in a mesh: inner: 16 (over y_hi, x, core), bulk: 16 (over z, y_lo).
Axes of the slice: x: 4, y: 4 (y_hi: 2, y_lo: 2; y = y_hi * 2 + y_lo), z: 8, core: 2. Of those that a mesh axis runs over, the one named last changes fastest.
Arguments:
- trajectory: float32 [128, 2097152], P(None, ('inner', 'bulk')), may hold values from -6 to 6
- targets: int32 [2097152], P(('inner', 'bulk')), may hold values from 0 to 131071, as said below
- remap_weights: float32 [2097152], P(('inner', 'bulk')), may hold values from 0.2 to 1
- legendre: float32 [256, 256, 256], P('inner'), may hold values from -0.375 to 0.375
- spectral_coef: float32 [128, 256], P('bulk'), may hold values from 0.2 to 2
Outputs:
- increment: float32 [128, 2097152], P(None, ('inner', 'bulk'))
The draws below stay inside these ranges and needn't reach their ends.
Inputs may be any that keep to these rules, and one draw needn't show every extreme that they name: `targets`: the fine points of device block k (points k * 8192 to (k + 1) * 8192 - 1, band i = k // 16) map to cells whose latitude lies within max(0, i * 16 - 8) and min(256, (i + 1) * 16 + 8) - 1; every such block reaches both ends of its latitude range.
All inputs are finite; a program needn't handle non-finite values.
Results may differ from the reference program's by a relative error of at most 0.00007.
Values sent between devices are 32-bit elements; how exact they have to be, the bound alone decides.
No kernel may reach another device: no remote copies, remote signals or barrier semaphores. Data moves between devices by JAX's collectives and lax.ppermute only.
A program may use at most 128 MiB of HBM per device.

```python
import math
import jax
import jax.numpy as jnp
from jax import lax

NLAT = 256
NLON = 512
M = 256
HP_DEV = 8192
LEV = 128
BAND = 16
RIM = 8
HPTS = 2097152
N_BULK = 16


def draw_targets(key, part):
    key = jax.random.fold_in(key, 11)
    key_lat, key_lon = jax.random.split(key)
    points = jnp.arange(HPTS, dtype=jnp.int32)
    band_index = points // HP_DEV // N_BULK
    low_row = jnp.maximum(0, band_index * BAND - RIM)
    high_row = jnp.minimum(NLAT, (band_index + 1) * BAND + RIM)
    lat = jax.random.randint(key_lat, (HPTS,), low_row, high_row)
    lon = jax.random.randint(key_lon, (HPTS,), 0, NLON)
    within = points % HP_DEV
    lat = jnp.where(within == 0, low_row, jnp.where(within == 1, high_row - 1, lat))
    lon = jnp.where(within == 0, 0, jnp.where(within == 1, NLON - 1, lon))
    return (lat * NLON + lon).astype(jnp.int32)


def block_levels(key, dims, cuts, least, high):
    def one(dim, shards_of):
        steps = jax.random.uniform(jax.random.fold_in(jax.random.fold_in(key, 6), dim), (shards_of,), jnp.float32, least / len(cuts), high / len(cuts))
        return jnp.repeat(jnp.exp(steps), dims[dim] // shards_of).reshape((-1,) + (1,) * (len(dims) - dim - 1))

    gain = one(*cuts[0])
    for cut in cuts[1:]:
        gain = gain * one(*cut)
    return gain


def normal_values(rng, extent, spread, most, cuts=(), held_as=jnp.bfloat16):
    result = jax.random.normal(rng, extent, jnp.float32) * spread
    if len(cuts) > 0:
        result = block_levels(rng, extent, cuts, -0.22, 0.18) * result
    return jnp.clip(result, min=-most, max=most).astype(held_as)


def setup_inputs(seed: int = 0) -> dict:
    splits = jax.random.split(jax.random.key(seed), 6)
    return {
        "trajectory": normal_values(splits[0], (LEV, HPTS), 1.0, 6.0, ((1, 256),), jnp.float32),
        "targets": draw_targets(jax.random.fold_in(splits[5], 71), 0),
        "remap_weights": jnp.clip(jnp.exp(math.log(1.0) - 1.609438 * jax.random.uniform(splits[2], (HPTS,), jnp.float32) ** block_levels(splits[2], (HPTS,), ((0, 256),), -0.2, 0.2)), 0.2, 1.0),
        "legendre": normal_values(splits[3], (M, NLAT, M), NLAT ** -0.5, 0.375, ((0, 16),), jnp.float32),
        "spectral_coef": jnp.clip(jnp.exp(math.log(2.0) - 2.3025851 * jax.random.uniform(splits[4], (LEV, M), jnp.float32) ** block_levels(splits[4], (LEV, M), ((0, 16),), -0.2, 0.2)), 0.2, 2.0),
    }


def fourier_table():
    lon = jnp.arange(NLON, dtype=jnp.int32)
    wave = jnp.arange(M, dtype=jnp.int32)
    phase = (wave[:, None] * lon[None, :] % NLON).astype(jnp.float32)
    angle = phase * (2.0 * jnp.pi / NLON)
    scale = 1.0 / jnp.sqrt(jnp.float32(NLON))
    return jnp.stack([jnp.cos(angle) * scale, -jnp.sin(angle) * scale])

def reference(trajectory, targets, remap_weights, legendre, spectral_coef):
    weighted = trajectory * remap_weights[None, :]
    coarse = jnp.zeros((LEV, NLAT * NLON), jnp.float32).at[:, targets].add(weighted)
    coarse = coarse.reshape(LEV, NLAT, NLON)
    table = fourier_table()
    fourier = jnp.einsum('alx,cmx->mcal', coarse, table, precision=lax.Precision.HIGHEST)
    wave = jnp.arange(M, dtype=jnp.int32)
    tri = (wave[None, :] >= wave[:, None]).astype(jnp.float32)
    masked = legendre * tri[:, None, :]
    spec = jnp.einsum('mcal,mln->mcan', fourier, masked, precision=lax.Precision.HIGHEST)
    spec = spec * spectral_coef[None, None, :, :]
    back = jnp.einsum('mcan,mln->mcal', spec, masked, precision=lax.Precision.HIGHEST)
    field = jnp.einsum('mcal,cmx->alx', back, table, precision=lax.Precision.HIGHEST)
    flat = field.reshape(LEV, NLAT * NLON)
    return flat[:, targets] * remap_weights[None, :]
```

```python
import functools

import jax
import jax.numpy as jnp
import ml_dtypes
import numpy as np
from jax import lax
from jax.experimental import pallas as pl
from jax.experimental.pallas import tpu as pltpu
from jax.sharding import PartitionSpec as P

NLAT = 256
NLON = 512
M = 256
LEV = 128
PTS = 8192
GROUP = 8 * NLON
CELLS = 4 * GROUP
HALF = 3 * GROUP // 2
CHAINS = 4
BLK = 128

EVEN = (2, 1, 0, 3)
ODD = (1, 2, 3, 0)


def tables():
    wave = np.arange(M)
    lon = np.arange(NLON)
    angle = 2.0 * np.pi * ((wave[None, :] * lon[:, None]) % NLON) / NLON
    both = np.stack([np.cos(angle), -np.sin(angle)], axis=-1) / np.sqrt(NLON)
    full = both.reshape(NLON, 2 * M).astype(np.float32)
    high = full.astype(ml_dtypes.bfloat16)
    low = (full - high.astype(np.float32)).astype(ml_dtypes.bfloat16)
    return high, low


def halves(value):
    high = value.astype(jnp.bfloat16)
    low = (value - high.astype(jnp.float32)).astype(jnp.bfloat16)
    return high, low


def split_dot(left, right, dims=(((1,), (0,)), ((), ()))):
    dot = functools.partial(
        lax.dot_general, dimension_numbers=dims, preferred_element_type=jnp.float32
    )
    return dot(left[0], right[0]) + (dot(left[0], right[1]) + dot(left[1], right[0]))


def place(core, group):
    return pl.multiple_of(jnp.where(core == 0, EVEN[group], ODD[group]) * GROUP, GROUP)


def level_block(z, y, part):
    row = lax.rem(z + part // 2, 8) * 2 + lax.rem(y + part % 2, 2)
    return pl.multiple_of(row * 8, 8)


def remap_kernel(
    where_ref, t_ref, x_hbm, w_ref,
    far_p, far_m, near, y1, y2, y3, y4, keep, cross,
    x_ref, first, second, third, in_sem, out_sem, *work,
):
    totals, turned = work[:CHAINS], work[CHAINS:]
    core, z, y = where_ref[0], where_ref[1], where_ref[2]
    loads = []
    for part in range(16):
        load = pltpu.make_async_copy(
            x_hbm.at[pl.ds(level_block(z, y, part), 8), :],
            x_ref.at[pl.ds(part * 8, 8), :],
            in_sem.at[part],
        )
        load.start()
        loads.append(load)
    zero = jnp.zeros((256, 128), jnp.float32)

    @pl.loop(0, CELLS // 256)
    def _(i):
        for total in totals:
            total[pl.ds(i * 256, 256), :] = zero

    for load in loads:
        load.wait()
    share = PTS // CHAINS

    @pl.loop(0, share // BLK)
    def _(b):
        for q in range(CHAINS):
            at = pl.multiple_of(q * share + b * BLK, BLK)
            turned[q][...] = (x_ref[:, pl.ds(at, BLK)] * w_ref[:, pl.ds(at, BLK)]).T
        for u in range(BLK):
            for q in range(CHAINS):
                cell = t_ref[q * share + b * BLK + u]
                totals[q][pl.ds(cell, 1), :] += turned[q][pl.ds(u, 1), :]

    def summed(start):
        value = totals[0][pl.ds(start, 128), :] + totals[1][pl.ds(start, 128), :]
        other = totals[2][pl.ds(start, 128), :] + totals[3][pl.ds(start, 128), :]
        return (value + other).T

    def fill(target, group, source, count, to):
        base = place(core, group) + source

        @pl.loop(0, count // 512)
        def _(i):
            for j in range(4):
                at = pl.multiple_of(base + i * 512 + j * 128, 128)
                block = summed(at).reshape(16, 8, 128)
                target[:, :, pl.ds(pl.multiple_of(to + i * 512 + j * 128, 128), 128)] = block

    copies = []

    def send(source, target):
        copy = pltpu.make_async_copy(source, target, out_sem.at[len(copies)])
        copy.start()
        copies.append(copy)

    fill(third, 3, 0, GROUP, 0)
    send(third, cross)
    fill(first, 1, GROUP // 2, GROUP // 2, 0)
    fill(first, 2, 0, GROUP, GROUP // 2)
    send(first.at[8], far_p)
    send(first.at[9], far_m)
    send(first.at[pl.ds(0, 8)], near.at[pl.ds(0, 8)])
    send(first.at[pl.ds(10, 6)], near.at[pl.ds(8, 6)])
    fill(second, 0, 0, GROUP, 0)
    fill(second, 1, 0, GROUP // 2, GROUP)
    for target, ks in ((y1, (4,)), (y2, (3, 5)), (y3, (2, 6)), (y4, (1, 7, 0))):
        for i, k in enumerate(ks):
            send(second.at[2 * k + 1], target.at[i])
    for k in range(8):
        send(second.at[2 * k], keep.at[k])
    for copy in copies:
        copy.wait()


def remap(where, cells, trajectory, weights):
    f32 = lambda *shape: jax.ShapeDtypeStruct(shape, jnp.float32)
    anywhere = pl.BlockSpec(memory_space=pl.ANY)
    smem = pl.BlockSpec(memory_space=pltpu.SMEM)
    return pl.pallas_call(
        remap_kernel,
        out_shape=[
            f32(8, HALF), f32(8, HALF), f32(14, 8, HALF),
            f32(1, 8, HALF), f32(2, 8, HALF), f32(2, 8, HALF), f32(3, 8, HALF),
            f32(8, 8, HALF), f32(16, 8, GROUP),
        ],
        in_specs=[smem, smem, anywhere, pl.BlockSpec(memory_space=pltpu.VMEM)],
        out_specs=[anywhere] * 9,
        scratch_shapes=[
            pltpu.VMEM((LEV, PTS), jnp.float32),
            pltpu.VMEM((16, 8, HALF), jnp.float32),
            pltpu.VMEM((16, 8, HALF), jnp.float32),
            pltpu.VMEM((16, 8, GROUP), jnp.float32),
            pltpu.SemaphoreType.DMA((16,)),
            pltpu.SemaphoreType.DMA((24,)),
        ]
        + [pltpu.VMEM((CELLS, 128), jnp.float32)] * CHAINS
        + [pltpu.VMEM((BLK, 128), jnp.float32)] * CHAINS,
        compiler_params=pltpu.CompilerParams(vmem_limit_bytes=56 * 2**20),
    )(where, cells, trajectory, weights)


def fetch_kernel(sources, *refs):
    where_ref, t_ref, w_ref = refs[:3]
    pieces = refs[3 : 3 + sum(len(s) > 0 for s in sources)]
    out_hbm = refs[3 + len(pieces)]
    flat, rows, out, in_sem, out_sem = refs[4 + len(pieces) : 9 + len(pieces)]
    turned = refs[9 + len(pieces) :]
    core, z, y = where_ref[0], where_ref[1], where_ref[2]
    loads = []
    for piece, spans in zip(pieces, sources):
        for lead, part, source, width, to in spans:
            view = piece if lead is None else piece.at[lead]
            load = pltpu.make_async_copy(
                view.at[:, pl.ds(source, width)],
                flat.at[part, :, pl.ds(to, width)],
                in_sem.at[len(loads)],
            )
            load.start()
            loads.append(load)
    for load in loads:
        load.wait()
    for group in range(4):
        base = place(core, group)

        @pl.loop(0, GROUP // 512)
        def _(i):
            for j in range(4):
                at = pl.multiple_of(group * GROUP + i * 512 + j * 128, 128)
                block = flat[:, :, pl.ds(at, 128)].reshape(128, 128)
                rows[pl.ds(pl.multiple_of(base + i * 512 + j * 128, 128), 128), :] = block.T

    @pl.loop(0, PTS // (4 * BLK))
    def _(b):
        for q in range(4):
            at = pl.multiple_of(b * 4 * BLK + q * BLK, BLK)
            for u in range(BLK):
                cell = t_ref[at + u]
                turned[q][pl.ds(u, 1), :] = rows[pl.ds(cell, 1), :]
            out[:, pl.ds(at, BLK)] = turned[q][...].T * w_ref[:, pl.ds(at, BLK)]

    stores = []
    for part in range(16):
        store = pltpu.make_async_copy(
            out.at[pl.ds(part * 8, 8), :],
            out_hbm.at[pl.ds(level_block(z, y, part), 8), :],
            out_sem.at[part],
        )
        store.start()
        stores.append(store)
    for store in stores:
        store.wait()


def fetch(where, cells, weights, pieces, sources):
    anywhere = pl.BlockSpec(memory_space=pl.ANY)
    smem = pl.BlockSpec(memory_space=pltpu.SMEM)
    count = sum(len(s) for s in sources)
    return pl.pallas_call(
        functools.partial(fetch_kernel, sources),
        out_shape=jax.ShapeDtypeStruct((LEV, PTS), jnp.float32),
        in_specs=[smem, smem, pl.BlockSpec(memory_space=pltpu.VMEM)] + [anywhere] * len(pieces),
        out_specs=anywhere,
        scratch_shapes=[
            pltpu.VMEM((16, 8, CELLS), jnp.float32),
            pltpu.VMEM((CELLS, 128), jnp.float32),
            pltpu.VMEM((LEV, PTS), jnp.float32),
            pltpu.SemaphoreType.DMA((count,)),
            pltpu.SemaphoreType.DMA((16,)),
        ]
        + [pltpu.VMEM((BLK, 128), jnp.float32)] * 4,
        compiler_params=pltpu.CompilerParams(vmem_limit_bytes=40 * 2**20),
    )(where, cells, weights, *pieces)


def keep_columns(target, value):
    for c in range(target.shape[0]):
        target[c] = value[:, c * 128 : (c + 1) * 128]


def every(source, start, count, stride):
    return jnp.concatenate(
        [source[c, pl.ds(start, count, stride=stride), :] for c in range(source.shape[0])], axis=1
    )


def forward_kernel(b_ref, a_ref, high_ref, low_ref, o_ref, work):
    rows = [b_ref[:, r * NLON : (r + 1) * NLON] for r in range(12)]
    rows += [a_ref[:, r * NLON : (r + 1) * NLON] for r in range(12)]
    left = halves(jnp.concatenate(rows, axis=0))
    keep_columns(work, split_dot(left, (high_ref[...], low_ref[...])))
    for a in range(8):
        lines = every(work, a, 24, 8)
        for i in range(16):
            o_ref[i, :, a * 32 : (a + 1) * 32] = lines[:, i * 32 : (i + 1) * 32]


def forward(b, a, high, low):
    return pl.pallas_call(
        forward_kernel,
        out_shape=jax.ShapeDtypeStruct((16, 24, 256), jnp.float32),
        scratch_shapes=[pltpu.VMEM((4, 192, 128), jnp.float32)],
    )(b, a, high, low)


def legendre_kernel(first_ref, x_ref, leg_ref, coef_ref, o_ref, lines, back):
    bands = []
    for i in range(16):
        inner, outer = x_ref[i, 0:8], x_ref[i, 8:16]
        if i % 2 == 0:
            if i > 0:
                outer = outer + x_ref[i - 1, 16:24]
            bands += [outer, inner]
        else:
            if i < 15:
                outer = outer + x_ref[i + 1, 16:24]
            bands += [inner, outer]
    keep_columns(lines, jnp.concatenate(bands, axis=0).T)
    coef = jnp.concatenate([coef_ref[...]] * 2, axis=0)
    total = lax.broadcasted_iota(jnp.int32, (16, 256), 1)
    for m in range(16):
        left = jnp.concatenate(
            [every(lines, 2 * m, 8, 32), every(lines, 2 * m + 1, 8, 32)], axis=0
        )
        table = halves(leg_ref[m])
        spec = split_dot(halves(left), table)
        spec = jnp.where(total >= first_ref[0] + m, spec * coef, 0.0)
        result = split_dot(halves(spec), table, (((1,), (1,)), ((), ())))
        for c in range(2):
            part = result[:, c * 128 : (c + 1) * 128]
            back[c, pl.ds(2 * m, 8, stride=32), :] = part[:8]
            back[c, pl.ds(2 * m + 1, 8, stride=32), :] = part[8:]
    whole = jnp.concatenate([back[c].T for c in range(2)], axis=0)
    nothing = jnp.zeros((8, 256), jnp.float32)
    for i in range(16):
        low, top = whole[16 * i : 16 * i + 8], whole[16 * i + 8 : 16 * i + 16]
        if i % 2 == 0:
            rim = whole[16 * i - 8 : 16 * i] if i > 0 else nothing
            parts = [top, low, rim]
        else:
            rim = whole[16 * i + 16 : 16 * i + 24] if i < 15 else nothing
            parts = [low, top, rim]
        o_ref[i] = jnp.concatenate(parts, axis=0)


def spectral(first, x, leg, coef):
    vmem = pl.BlockSpec(memory_space=pltpu.VMEM)
    return pl.pallas_call(
        legendre_kernel,
        out_shape=jax.ShapeDtypeStruct((16, 24, 256), jnp.float32),
        in_specs=[pl.BlockSpec(memory_space=pltpu.SMEM), vmem, vmem, vmem],
        scratch_shapes=[pltpu.VMEM((2, 256, 128), jnp.float32)] * 2,
        compiler_params=pltpu.CompilerParams(vmem_limit_bytes=24 * 2**20),
    )(first, x, leg, coef)


def inverse_kernel(x_ref, high_ref, low_ref, a_ref, b_ref, work, lines):
    for a in range(8):
        for i in range(16):
            work[a * 24 : (a + 1) * 24, i * 32 : (i + 1) * 32] = x_ref[i, :, a * 32 : (a + 1) * 32]
    table = (high_ref[...], low_ref[...])
    keep_columns(lines, split_dot(halves(work[...]), table, (((1,), (1,)), ((), ()))))
    for r in range(24):
        out = a_ref if r < 12 else b_ref
        at = (r % 12) * NLON
        out[:, at : at + NLON] = every(lines, r, 8, 24)


def inverse(x, high, low):
    half = jax.ShapeDtypeStruct((8, HALF), jnp.float32)
    return pl.pallas_call(
        inverse_kernel,
        out_shape=[half, half],
        scratch_shapes=[pltpu.VMEM((192, 512), jnp.float32), pltpu.VMEM((4, 192, 128), jnp.float32)],
    )(x, high, low)


ALONG = [(b, (b + 2) % 16) for b in range(16)]
AGAINST = [(b, (b - 2) % 16) for b in range(16)]
ACROSS = [(b, b ^ 1) for b in range(16)]


def ahead(x):
    return lax.ppermute(x, "bulk", ALONG)


def behind(x):
    return lax.ppermute(x, "bulk", AGAINST)


def across(x):
    return lax.ppermute(x, "bulk", ACROSS)


def other_core(x):
    return lax.ppermute(x, "inner", ACROSS)


def gather_sums(far_p, far_m, near, y1, y2, y3, y4, keep, cross):
    ks = {0: 0, 1: 2, 2: 4, 3: 6, 5: 8, 6: 10, 7: 12}
    own = lambda k: near[ks[k] : ks[k] + 2]
    shared = other_core(cross)
    plus, minus = ahead(far_p), behind(far_m)

    def with_core(piece, order, r):
        add = jnp.stack([shared[2 * k + r] for k in order])
        return jnp.concatenate([piece[:, :, :GROUP] + add, piece[:, :, GROUP:]], axis=2)

    got = [
        across(with_core(piece, order, 1))
        for piece, order in ((y1, (4,)), (y2, (3, 5)), (y3, (2, 6)), (y4, (1, 7, 0)))
    ]
    mine = with_core(keep, tuple(range(8)), 0)
    b = {4: mine[4] + got[0][0]}
    b_plus, b_minus = ahead(b[4][:, : HALF // 2]), behind(b[4][:, HALF // 2 :])
    plus = ahead(jnp.stack([own(3)[0] + plus, own(3)[1]]))
    minus = behind(jnp.stack([own(5)[0], own(5)[1] + minus]))
    b[3], b[5] = mine[3] + got[1][0], mine[5] + got[1][1]
    b_plus = ahead(jnp.concatenate([b[3][:, : HALF // 2] + b_plus, b[3][:, HALF // 2 :]], 1))
    b_minus = behind(jnp.concatenate([b[5][:, : HALF // 2], b[5][:, HALF // 2 :] + b_minus], 1))
    plus, minus = ahead(own(2) + plus), behind(own(6) + minus)
    b_plus, b_minus = (
        ahead(mine[2] + got[2][0] + b_plus),
        behind(mine[6] + got[2][1] + b_minus),
    )
    plus, minus = ahead(own(1) + plus), behind(own(7) + minus)
    b_plus, b_minus = (
        ahead(mine[1] + got[3][0] + b_plus),
        behind(mine[7] + got[3][1] + b_minus),
    )
    a = own(0) + plus + minus
    a = a[0] + across(a[1])
    return mine[0] + got[3][2] + b_plus + b_minus, a


def spread_field(a, b):
    pieces, sources = [], []

    def give(piece, *spans):
        pieces.append(piece)
        sources.append(spans)

    def pair(piece, k):
        give(piece, (0, 2 * k, 0, HALF, 0), (1, 2 * k + 1, 0, HALF, 0))

    def one(piece, k, r, lead=None):
        give(piece, (lead, 2 * k + r, 0, HALF, HALF))

    own = jnp.concatenate([a, b], axis=1)
    other = across(own)
    mine = jnp.stack([a, other[:, :HALF]])
    plus, minus = mine, mine
    b_plus, b_minus = b, b
    pair(mine, 0)
    one(b, 0, 0)
    give(other, (None, 1, HALF, HALF, HALF))
    core = [mine[:, :, :GROUP]]
    order = [0]
    for step in (1, 2, 3):
        b_plus, b_minus = ahead(b_plus), behind(b_minus)
        plus, minus = ahead(plus), behind(minus)
        pair(plus, 8 - step)
        pair(minus, step)
        one(b_plus, 8 - step, 0)
        one(b_minus, step, 0)
        both = across(jnp.stack([b_plus, b_minus]))
        give(
            both,
            (0, 2 * (8 - step) + 1, 0, HALF, HALF),
            (1, 2 * step + 1, 0, HALF, HALF),
        )
        core += [plus[:, :, :GROUP], minus[:, :, :GROUP]]
        order += [8 - step, step]
    last = jnp.concatenate(
        [ahead(b_plus[:, : HALF // 2]), behind(b_minus[:, HALF // 2 :])], axis=1
    )
    far_p, far_m = ahead(plus[0]), behind(minus[1])
    give(far_p, (None, 8, 0, HALF, 0))
    give(far_m, (None, 9, 0, HALF, 0))
    one(last, 4, 0)
    one(across(last), 4, 1)
    early = other_core(jnp.concatenate(core[:5], axis=0))
    late = other_core(
        jnp.concatenate(core[5:] + [far_p[None, :, :GROUP], far_m[None, :, :GROUP]], axis=0)
    )
    order += [4]
    spans = [
        (2 * n + r, 2 * k + r, 0, GROUP, 3 * GROUP) for n, k in enumerate(order) for r in (0, 1)
    ]
    give(early, *spans[:10])
    give(late, *[(lead - 10,) + rest for lead, *rest in map(tuple, spans[10:]) for rest in [tuple(rest)]])
    return pieces, sources


def shards(trajectory, targets, remap_weights, legendre, spectral_coef):
    inner = lax.axis_index("inner")
    bulk = lax.axis_index("bulk")
    where = jnp.stack([inner % 2, bulk // 2, bulk % 2]).astype(jnp.int32)
    cells = targets - (inner * 16 - 8) * NLON
    weights = remap_weights[None, :]
    high, low = (jnp.asarray(t) for t in tables())
    b, a = gather_sums(*remap(where, cells, trajectory, weights))
    sent = lax.all_to_all(forward(b, a, high, low), "inner", 0, 0, tiled=True)
    first = (inner * 16).astype(jnp.int32)[None]
    back = spectral(first, sent, legendre, spectral_coef)
    back = lax.all_to_all(back, "inner", 0, 0, tiled=True)
    pieces, sources = spread_field(*inverse(back, high, low))
    return fetch(where, cells, weights, pieces, sources)


def solution(mesh):
    placed = (
        P(None, ("inner", "bulk")),
        P(("inner", "bulk")),
        P(("inner", "bulk")),
        P("inner", None, None),
        P("bulk", None),
    )
    return jax.shard_map(
        shards, mesh=mesh, in_specs=placed, out_specs=P(None, ("inner", "bulk")), check_vma=False
    )
```

```python
import functools

import jax
import jax.numpy as jnp
import ml_dtypes
import numpy as np
from jax import lax
from jax.experimental import pallas as pl
from jax.experimental.pallas import tpu as pltpu
from jax.sharding import PartitionSpec as P

NLAT = 256
NLON = 512
M = 256
LEV = 128
PTS = 8192
GROUP = 8 * NLON
CELLS = 4 * GROUP
HALF = 3 * GROUP // 2
CHAINS = 4
BLK = 128
NEAR = (0, 1, 2, 3, 5, 6, 7)
REST = tuple(2 * k + r for k in NEAR for r in (0, 1))

EVEN = (1, 0, 3, 2)
ODD = (2, 3, 0, 1)


def tables():
    wave = np.arange(M)
    lon = np.arange(NLON)
    angle = 2.0 * np.pi * ((wave[None, :] * lon[:, None]) % NLON) / NLON
    both = np.stack([np.cos(angle), -np.sin(angle)], axis=-1) / np.sqrt(NLON)
    full = both.reshape(NLON, 2 * M).astype(np.float32)
    high = full.astype(ml_dtypes.bfloat16)
    low = (full - high.astype(np.float32)).astype(ml_dtypes.bfloat16)
    return high, low


def halves(value):
    high = value.astype(jnp.bfloat16)
    low = (value - high.astype(jnp.float32)).astype(jnp.bfloat16)
    return high, low


def split_dot(left, right, dims=(((1,), (0,)), ((), ()))):
    dot = functools.partial(
        lax.dot_general, dimension_numbers=dims, preferred_element_type=jnp.float32
    )
    return dot(left[0], right[0]) + (dot(left[0], right[1]) + dot(left[1], right[0]))


def place(core, group):
    return pl.multiple_of(jnp.where(core == 0, EVEN[group], ODD[group]) * GROUP, GROUP)


def level_block(z, y, part):
    row = lax.rem(z + part // 2, 8) * 2 + lax.rem(y + part % 2, 2)
    return pl.multiple_of(row * 8, 8)


def remap_kernel(
    where_ref, t_ref, x_hbm, w_ref,
    *refs,
):
    outs, (x_ref, in_sem, *work) = refs[:23], refs[23:]
    totals, turned = work[:CHAINS], work[CHAINS:]
    core, z, y = where_ref[0], where_ref[1], where_ref[2]
    loads = []
    for part in range(16):
        load = pltpu.make_async_copy(
            x_hbm.at[pl.ds(level_block(z, y, part), 8), :],
            x_ref.at[pl.ds(part * 8, 8), :],
            in_sem.at[part],
        )
        load.start()
        loads.append(load)
    zero = jnp.zeros((256, 128), jnp.float32)

    @pl.loop(0, CELLS // 256)
    def _(i):
        for total in totals:
            total[pl.ds(i * 256, 256), :] = zero

    for load in loads:
        load.wait()
    share = PTS // CHAINS

    @pl.loop(0, share // (4 * BLK))
    def _(b):
        for n in range(4):
            for q in range(CHAINS):
                at = pl.multiple_of(q * share + (4 * b + n) * BLK, BLK)
                turned[4 * q + n][...] = (x_ref[:, pl.ds(at, BLK)] * w_ref[:, pl.ds(at, BLK)]).T
            for u in range(BLK):
                for q in range(CHAINS):
                    cell = t_ref[q * share + (4 * b + n) * BLK + u] & (CELLS - 1)
                    totals[q][pl.ds(cell, 1), :] += turned[4 * q + n][pl.ds(u, 1), :]

    def summed(start):
        value = totals[0][pl.ds(start, 128), :] + totals[1][pl.ds(start, 128), :]
        other = totals[2][pl.ds(start, 128), :] + totals[3][pl.ds(start, 128), :]
        return (value + other).T

    def fill(targets, group, source, count, to):
        base = place(core, group) + source

        @pl.loop(0, count // 512)
        def _(i):
            for j in range(4):
                step = i * 512 + j * 128
                block = summed(pl.multiple_of(base + step, 128))
                for part, (target, start) in targets.items():
                    at = pl.multiple_of(start + to + step, 128)
                    target[:, pl.ds(at, 128)] = block[part * 8 : part * 8 + 8]

    outs = iter(outs)

    def take(width, *lists):
        found = {}
        for parts in lists:
            target = next(outs)
            found.update({part: (target, n * width) for n, part in enumerate(parts)})
        return found

    third = take(GROUP, (8, 9), REST)
    second = take(HALF, (9,), (7, 11), (5, 13), (3, 15, 1), *[(2 * k,) for k in range(8)])
    first = take(HALF, (8,), (9,), *[(2 * k, 2 * k + 1) for k in NEAR])
    fill(third, 3, 0, GROUP, 0)
    fill(second, 0, 0, GROUP, 0)
    fill(second, 1, 0, GROUP // 2, GROUP)
    fill(first, 1, GROUP // 2, GROUP // 2, 0)
    fill(first, 2, 0, GROUP, GROUP // 2)


def remap(where, targets, trajectory, weights):
    f32 = lambda *shape: jax.ShapeDtypeStruct(shape, jnp.float32)
    smem = pl.BlockSpec(memory_space=pltpu.SMEM)
    vmem = pl.BlockSpec(memory_space=pltpu.VMEM)
    return pl.pallas_call(
        remap_kernel,
        out_shape=[f32(8, 2 * GROUP), f32(8, 14 * GROUP)]
        + [f32(8, n * HALF) for n in (1, 2, 2, 3)]
        + [f32(8, HALF)] * 10
        + [f32(8, 2 * HALF)] * 7,
        in_specs=[smem, smem, pl.BlockSpec(memory_space=pltpu.HBM), vmem],
        out_specs=[vmem] * 23,
        scratch_shapes=[
            pltpu.VMEM((LEV, PTS), jnp.float32),
            pltpu.SemaphoreType.DMA((16,)),
        ]
        + [pltpu.VMEM((CELLS, 128), jnp.float32)] * CHAINS
        + [pltpu.VMEM((BLK, 128), jnp.float32)] * (4 * CHAINS),
        compiler_params=pltpu.CompilerParams(vmem_limit_bytes=48 * 2**20),
    )(where, targets, trajectory, weights)


def fetch_kernel(sources, *refs):
    where_ref, t_ref, w_ref = refs[:3]
    pieces = refs[3 : 3 + len(sources)]
    out_hbm = refs[3 + len(sources)]
    rows, out, out_sem = refs[4 + len(sources) : 7 + len(sources)]
    turned = refs[7 + len(sources) :]
    core, z, y = where_ref[0], where_ref[1], where_ref[2]
    spans = [(part, to, width, piece, source) for piece, given in zip(pieces, sources)
             for part, source, width, to in given]
    for start, group, inside, width in (
        (0, 0, 0, GROUP),
        (GROUP, 1, 0, GROUP // 2),
        (HALF, 1, GROUP // 2, GROUP // 2),
        (HALF + GROUP // 2, 2, 0, GROUP),
        (3 * GROUP, 3, 0, GROUP),
    ):
        base = place(core, group) + inside
        found = {}
        for part, to, length, piece, source in spans:
            if to <= start and start + width <= to + length:
                found[part] = (piece, source + start - to)

        @pl.loop(0, width // 512)
        def _(i):
            for j in range(4):
                step = i * 512 + j * 128
                block = jnp.concatenate(
                    [
                        found[part][0][:, pl.ds(pl.multiple_of(found[part][1] + step, 128), 128)]
                        for part in range(16)
                    ],
                    axis=0,
                )
                rows[pl.ds(pl.multiple_of(base + step, 128), 128), :] = block.T

    share = PTS // 4
    stores = []
    for h in range(4):
        for q in range(share // BLK):
            at = h * share + q * BLK
            for u in range(BLK):
                cell = t_ref[at + u]
                turned[q][pl.ds(u, 1), :] = rows[pl.ds(cell, 1), :]
            out[:, pl.ds(at, BLK)] = turned[q][...].T * w_ref[:, pl.ds(at, BLK)]
        for part in range(16):
            store = pltpu.make_async_copy(
                out.at[pl.ds(part * 8, 8), pl.ds(h * share, share)],
                out_hbm.at[pl.ds(level_block(z, y, part), 8), pl.ds(h * share, share)],
                out_sem.at[h * 16 + part],
            )
            store.start()
            stores.append(store)
    for store in stores:
        store.wait()


def fetch(where, cells, weights, pieces, sources):
    smem = pl.BlockSpec(memory_space=pltpu.SMEM)
    vmem = pl.BlockSpec(memory_space=pltpu.VMEM)
    return pl.pallas_call(
        functools.partial(fetch_kernel, sources),
        out_shape=jax.ShapeDtypeStruct((LEV, PTS), jnp.float32),
        in_specs=[smem, smem] + [vmem] * (1 + len(pieces)),
        out_specs=pl.BlockSpec(memory_space=pl.ANY),
        scratch_shapes=[
            pltpu.VMEM((CELLS, 128), jnp.float32),
            pltpu.VMEM((LEV, PTS), jnp.float32),
            pltpu.SemaphoreType.DMA((64,)),
        ]
        + [pltpu.VMEM((BLK, 128), jnp.float32)] * 16,
        compiler_params=pltpu.CompilerParams(vmem_limit_bytes=40 * 2**20),
    )(where, cells, weights, *pieces)


def keep_columns(target, value):
    for c in range(target.shape[0]):
        target[c] = value[:, c * 128 : (c + 1) * 128]


def every(source, start, count, stride):
    return jnp.concatenate(
        [source[c, pl.ds(start, count, stride=stride), :] for c in range(source.shape[0])], axis=1
    )


def forward_kernel(b_ref, a_ref, high_ref, low_ref, o_ref, work):
    rows = [b_ref[:, r * NLON : (r + 1) * NLON] for r in range(12)]
    rows += [a_ref[:, r * NLON : (r + 1) * NLON] for r in range(12)]
    left = halves(jnp.concatenate(rows, axis=0))
    keep_columns(work, split_dot(left, (high_ref[...], low_ref[...])))
    for a in range(8):
        lines = every(work, a, 24, 8)
        for i in range(16):
            o_ref[i, :, a * 32 : (a + 1) * 32] = lines[:, i * 32 : (i + 1) * 32]


def forward(b, a, high, low):
    return pl.pallas_call(
        forward_kernel,
        out_shape=jax.ShapeDtypeStruct((16, 24, 256), jnp.float32),
        scratch_shapes=[pltpu.VMEM((4, 192, 128), jnp.float32)],
    )(b, a, high, low)


def legendre_kernel(first_ref, x_ref, high_ref, low_ref, coef_ref, o_ref, lines, back):
    bands = []
    for i in range(16):
        inner, outer = x_ref[i, 0:8], x_ref[i, 8:16]
        if i % 2 == 0:
            if i > 0:
                outer = outer + x_ref[i - 1, 16:24]
            bands += [outer, inner]
        else:
            if i < 15:
                outer = outer + x_ref[i + 1, 16:24]
            bands += [inner, outer]
    keep_columns(lines, jnp.concatenate(bands, axis=0).T)
    coef = jnp.concatenate([coef_ref[...]] * 2, axis=0)
    total = lax.broadcasted_iota(jnp.int32, (16, 256), 1)
    for m in range(16):
        left = jnp.concatenate(
            [every(lines, 2 * m, 8, 32), every(lines, 2 * m + 1, 8, 32)], axis=0
        )
        table = (high_ref[m], low_ref[m])
        spec = split_dot(halves(left), table)
        spec = jnp.where(total >= first_ref[0] + m, spec * coef, 0.0)
        result = split_dot(halves(spec), table, (((1,), (1,)), ((), ())))
        for c in range(2):
            part = result[:, c * 128 : (c + 1) * 128]
            back[c, pl.ds(2 * m, 8, stride=32), :] = part[:8]
            back[c, pl.ds(2 * m + 1, 8, stride=32), :] = part[8:]
    whole = jnp.concatenate([back[c].T for c in range(2)], axis=0)
    nothing = jnp.zeros((8, 256), jnp.float32)
    for i in range(16):
        low, top = whole[16 * i : 16 * i + 8], whole[16 * i + 8 : 16 * i + 16]
        if i % 2 == 0:
            rim = whole[16 * i - 8 : 16 * i] if i > 0 else nothing
            parts = [top, low, rim]
        else:
            rim = whole[16 * i + 16 : 16 * i + 24] if i < 15 else nothing
            parts = [low, top, rim]
        o_ref[i] = jnp.concatenate(parts, axis=0)


def spectral(first, x, table, coef):
    vmem = pl.BlockSpec(memory_space=pltpu.VMEM)
    return pl.pallas_call(
        legendre_kernel,
        out_shape=jax.ShapeDtypeStruct((16, 24, 256), jnp.float32),
        in_specs=[pl.BlockSpec(memory_space=pltpu.SMEM)] + [vmem] * 4,
        scratch_shapes=[pltpu.VMEM((2, 256, 128), jnp.float32)] * 2,
        compiler_params=pltpu.CompilerParams(vmem_limit_bytes=24 * 2**20),
    )(first, x, *table, coef)


def split_kernel(x_ref, high_ref, low_ref):
    @pl.loop(0, x_ref.shape[0])
    def _(m):
        high_ref[m], low_ref[m] = halves(x_ref[m])


def split_table(x):
    half = jax.ShapeDtypeStruct(x.shape, jnp.bfloat16)
    return pl.pallas_call(
        split_kernel,
        out_shape=[half, half],
        cost_estimate=pl.CostEstimate(
            flops=4 * x.size, bytes_accessed=8 * x.size, transcendentals=0
        ),
        compiler_params=pltpu.CompilerParams(vmem_limit_bytes=24 * 2**20),
    )(x)


def inverse_kernel(x_ref, high_ref, low_ref, a_ref, b_ref, work, lines):
    for a in range(8):
        for i in range(16):
            work[a * 24 : (a + 1) * 24, i * 32 : (i + 1) * 32] = x_ref[i, :, a * 32 : (a + 1) * 32]
    table = (high_ref[...], low_ref[...])
    keep_columns(lines, split_dot(halves(work[...]), table, (((1,), (1,)), ((), ()))))
    for r in range(24):
        out = a_ref if r < 12 else b_ref
        at = (r % 12) * NLON
        out[:, at : at + NLON] = every(lines, r, 8, 24)


def inverse(x, high, low):
    half = jax.ShapeDtypeStruct((8, HALF), jnp.float32)
    return pl.pallas_call(
        inverse_kernel,
        out_shape=[half, half],
        scratch_shapes=[pltpu.VMEM((192, 512), jnp.float32), pltpu.VMEM((4, 192, 128), jnp.float32)],
    )(x, high, low)


ALONG = [(b, (b + 2) % 16) for b in range(16)]
AGAINST = [(b, (b - 2) % 16) for b in range(16)]
ACROSS = [(b, b ^ 1) for b in range(16)]


def ahead(x):
    return lax.ppermute(x, "bulk", ALONG)


def behind(x):
    return lax.ppermute(x, "bulk", AGAINST)


def across(x):
    return lax.ppermute(x, "bulk", ACROSS)


def other_core(x):
    return lax.ppermute(x, "inner", ACROSS)


def together(*moves):
    hold = lax.optimization_barrier
    values = hold(tuple(value for _, value in moves))
    return hold(tuple(move(value) for (move, _), value in zip(moves, values)))


def wide(*blocks):
    return jnp.concatenate(blocks, axis=1)


def gather_sums(legendre, targets, cross_far, cross, y1, y2, y3, y4, *rest):
    keep, far_p, far_m = rest[:8], rest[8], rest[9]
    flat = lambda k: rest[10 + NEAR.index(k)]
    quarter = HALF // 2

    def with_core(piece, add):
        return wide(piece[:, :GROUP] + add, piece[:, GROUP:])

    def part_of(source, n, width):
        return source[:, n * width : (n + 1) * width]

    (shared_far,) = together((other_core, cross_far))
    p, m, y, shared = together(
        (ahead, far_p),
        (behind, far_m),
        (across, with_core(y1, part_of(shared_far, 1, GROUP))),
        (other_core, cross),
    )
    from_core = lambda k, r: (
        part_of(shared_far, r, GROUP)
        if k == 4
        else part_of(shared, 2 * NEAR.index(k) + r, GROUP)
    )
    mine = lambda k: with_core(keep[k], from_core(k, 0))
    send = lambda piece, *order: wide(
        *[with_core(part_of(piece, i, HALF), from_core(k, 1)) for i, k in enumerate(order)]
    )
    here = mine(4) + y
    p, m, y = together(
        (ahead, wide(flat(3) + wide(p, jnp.zeros_like(p)), here[:, :quarter])),
        (behind, wide(flat(5) + wide(jnp.zeros_like(m), m), here[:, quarter:])),
        (across, send(y2, 3, 5)),
    )
    here_p = mine(3) + y[:, :HALF]
    here_m = mine(5) + y[:, HALF:]
    here_p = wide(here_p[:, :quarter] + p[:, 2 * HALF :], here_p[:, quarter:])
    here_m = wide(here_m[:, :quarter], here_m[:, quarter:] + m[:, 2 * HALF :])
    p, m, y, table, cells = together(
        (ahead, wide(flat(2) + p[:, : 2 * HALF], here_p)),
        (behind, wide(flat(6) + m[:, : 2 * HALF], here_m)),
        (across, send(y3, 2, 6)),
        (split_table, legendre),
        (lambda t: t & (CELLS - 1), targets),
    )
    p, m, y = together(
        (ahead, wide(flat(1), mine(2) + y[:, :HALF]) + p),
        (behind, wide(flat(7), mine(6) + y[:, HALF:]) + m),
        (across, send(y4, 1, 7, 0)),
    )
    both = flat(0) + p[:, : 2 * HALF] + m[:, : 2 * HALF]
    own = mine(0) + y[:, 2 * HALF :]
    p, m, y = together(
        (ahead, mine(1) + y[:, :HALF] + p[:, 2 * HALF :]),
        (behind, mine(7) + y[:, HALF : 2 * HALF] + m[:, 2 * HALF :]),
        (across, both[:, HALF:]),
    )
    return own + p + m, both[:, :HALF] + y, table, cells


def spread_field(a, b):
    pieces, sources = [], []
    quarter = HALF // 2

    def give(piece, *spans):
        pieces.append(piece)
        sources.append(spans)

    def first(k, r, source):
        return (2 * k + r, source, HALF, 0)

    def second(k, r, source):
        return (2 * k + r, source, HALF, HALF)

    def all_of(k, source):
        return [second(k, 0, source), second(k, 1, source + HALF)]

    give(a, first(0, 0, 0))
    give(b, second(0, 0, 0))
    p, m, y = together((ahead, a), (behind, a), (across, b))
    give(y, second(0, 1, 0))
    near = [(0, a), (7, p), (1, m)]
    give(p, first(7, 0, 0))
    give(m, first(1, 0, 0))
    pair = wide(b, y)
    p, m, y = together(
        (ahead, wide(pair, p)), (behind, wide(pair, m)), (across, wide(a, p, m))
    )
    give(y, first(0, 1, 0), first(7, 1, HALF), first(1, 1, 2 * HALF))
    heads = [(1, y[:, :GROUP]), (15, y[:, HALF : HALF + GROUP]), (3, y[:, 2 * HALF : 2 * HALF + GROUP])]
    heads += [(2 * k, value[:, :GROUP]) for k, value in near]
    for step in (2, 3):
        give(p, *all_of(9 - step, 0), first(8 - step, 0, 2 * HALF))
        give(m, *all_of(step - 1, 0), first(step, 0, 2 * HALF))
        new_p, new_m = p[:, 2 * HALF :], m[:, 2 * HALF :]
        heads += [(2 * (8 - step), new_p[:, :GROUP]), (2 * step, new_m[:, :GROUP])]
        if step == 2:
            p, m, y = together((ahead, p), (behind, m), (across, wide(new_p, new_m)))
        else:
            p, m, y = together(
                (ahead, p[:, : 2 * HALF + quarter]),
                (behind, wide(m[:, : 2 * HALF], new_m[:, quarter:])),
                (across, wide(new_p, new_m)),
            )
        give(y, first(8 - step, 1, 0), first(step, 1, HALF))
        heads += [(2 * (8 - step) + 1, y[:, :GROUP]), (2 * step + 1, y[:, HALF : HALF + GROUP])]
    give(p, *all_of(5, 0))
    give(m, *all_of(3, 0))
    far = wide(p[:, 2 * HALF :], m[:, 2 * HALF :])
    give(far, first(4, 0, 0))
    heads += [(8, far[:, :GROUP])]
    p, m, y, core = together(
        (ahead, p[:, :HALF]),
        (behind, m[:, HALF : 2 * HALF]),
        (across, far),
        (other_core, wide(*[value for _, value in heads])),
    )
    give(p, second(4, 0, 0))
    give(m, second(4, 1, 0))
    give(y, first(4, 1, 0))
    give(core, *[(part, n * GROUP, GROUP, 3 * GROUP) for n, (part, _) in enumerate(heads)])
    (core,) = together((other_core, y[:, :GROUP]))
    give(core, (9, 0, GROUP, 3 * GROUP))
    return pieces, sources


def shards(trajectory, targets, remap_weights, legendre, spectral_coef):
    inner = lax.axis_index("inner")
    bulk = lax.axis_index("bulk")
    where = jnp.stack([inner % 2, bulk // 2, bulk % 2]).astype(jnp.int32)
    weights = remap_weights[None, :]
    high, low = (jnp.asarray(t) for t in tables())
    b, a, table, cells = gather_sums(legendre, targets, *remap(where, targets, trajectory, weights))
    sent = lax.all_to_all(forward(b, a, high, low), "inner", 0, 0, tiled=True)
    first = (inner * 16).astype(jnp.int32)[None]
    back = spectral(first, sent, table, spectral_coef)
    back = lax.all_to_all(back, "inner", 0, 0, tiled=True)
    pieces, sources = spread_field(*inverse(back, high, low))
    return fetch(where, cells, weights, pieces, sources)


def solution(mesh):
    placed = (
        P(None, ("inner", "bulk")),
        P(("inner", "bulk")),
        P(("inner", "bulk")),
        P("inner", None, None),
        P("bulk", None),
    )
    return jax.shard_map(
        shards, mesh=mesh, in_specs=placed, out_specs=P(None, ("inner", "bulk")), check_vma=False
    )
```

```python
import functools

import jax
import jax.numpy as jnp
import ml_dtypes
import numpy as np
from jax import lax
from jax.experimental import pallas as pl
from jax.experimental.pallas import tpu as pltpu
from jax.sharding import PartitionSpec as P

NLAT = 256
NLON = 512
M = 256
LEV = 128
PTS = 8192
GROUP = 8 * NLON
CELLS = 4 * GROUP
HALF = 3 * GROUP // 2
CHAINS = 4
BLK = 128
NEAR = (0, 1, 2, 3, 5, 6, 7)
FAR = tuple(2 * k + r for k in (4, 3, 5) for r in (0, 1))
REST = tuple(2 * k + r for k in (2, 6, 1, 7, 0) for r in (0, 1))

EVEN = (1, 0, 3, 2)
ODD = (2, 3, 0, 1)


def tables():
    wave = np.arange(M)
    lon = np.arange(NLON)
    angle = 2.0 * np.pi * ((wave[None, :] * lon[:, None]) % NLON) / NLON
    both = np.stack([np.cos(angle), -np.sin(angle)], axis=-1) / np.sqrt(NLON)
    full = both.reshape(NLON, 2 * M).astype(np.float32)
    high = full.astype(ml_dtypes.bfloat16)
    low = (full - high.astype(np.float32)).astype(ml_dtypes.bfloat16)
    return high, low


def halves(value):
    high = value.astype(jnp.bfloat16)
    low = (value - high.astype(jnp.float32)).astype(jnp.bfloat16)
    return high, low


def split_dot(left, right, dims=(((1,), (0,)), ((), ()))):
    dot = functools.partial(
        lax.dot_general, dimension_numbers=dims, preferred_element_type=jnp.float32
    )
    return dot(left[0], right[0]) + (dot(left[0], right[1]) + dot(left[1], right[0]))


def place(core, group):
    return pl.multiple_of(jnp.where(core == 0, EVEN[group], ODD[group]) * GROUP, GROUP)


def level_block(z, y, part):
    row = lax.rem(z + part // 2, 8) * 2 + lax.rem(y + part % 2, 2)
    return pl.multiple_of(row * 8, 8)


def remap_kernel(
    where_ref, t_ref, x_hbm, w_ref,
    *refs,
):
    outs, (x_ref, in_sem, *work) = refs[:23], refs[23:]
    totals, turned = work[:CHAINS], work[CHAINS:]
    core, z, y = where_ref[0], where_ref[1], where_ref[2]
    loads = []
    for part in range(16):
        load = pltpu.make_async_copy(
            x_hbm.at[pl.ds(level_block(z, y, part), 8), :],
            x_ref.at[pl.ds(part * 8, 8), :],
            in_sem.at[part],
        )
        load.start()
        loads.append(load)
    zero = jnp.zeros((256, 128), jnp.float32)

    @pl.loop(0, CELLS // 256)
    def _(i):
        for total in totals:
            total[pl.ds(i * 256, 256), :] = zero

    for load in loads:
        load.wait()
    share = PTS // CHAINS

    @pl.loop(0, share // (4 * BLK))
    def _(b):
        for n in range(4):
            for q in range(CHAINS):
                at = pl.multiple_of(q * share + (4 * b + n) * BLK, BLK)
                turned[4 * q + n][...] = (x_ref[:, pl.ds(at, BLK)] * w_ref[:, pl.ds(at, BLK)]).T
            for u in range(BLK):
                for q in range(CHAINS):
                    cell = t_ref[q * share + (4 * b + n) * BLK + u] & (CELLS - 1)
                    totals[q][pl.ds(cell, 1), :] += turned[4 * q + n][pl.ds(u, 1), :]

    def summed(start):
        value = totals[0][pl.ds(start, 128), :] + totals[1][pl.ds(start, 128), :]
        other = totals[2][pl.ds(start, 128), :] + totals[3][pl.ds(start, 128), :]
        return (value + other).T

    def fill(targets, group, source, count, to):
        base = place(core, group) + source

        @pl.loop(0, count // 512)
        def _(i):
            for j in range(4):
                step = i * 512 + j * 128
                block = summed(pl.multiple_of(base + step, 128))
                for part, (target, start) in targets.items():
                    at = pl.multiple_of(start + to + step, 128)
                    target[:, pl.ds(at, 128)] = block[part * 8 : part * 8 + 8]

    outs = iter(outs)

    def take(width, *lists):
        found = {}
        for parts in lists:
            target = next(outs)
            found.update({part: (target, n * width) for n, part in enumerate(parts)})
        return found

    third = take(GROUP, FAR, REST)
    second = take(HALF, (9,), (7, 11), (5, 13), (3, 15, 1), *[(2 * k,) for k in range(8)])
    first = take(HALF, (8,), (9,), *[(2 * k, 2 * k + 1) for k in NEAR])
    fill(third, 3, 0, GROUP, 0)
    fill(second, 0, 0, GROUP, 0)
    fill(second, 1, 0, GROUP // 2, GROUP)
    fill(first, 1, GROUP // 2, GROUP // 2, 0)
    fill(first, 2, 0, GROUP, GROUP // 2)


def remap(where, targets, trajectory, weights):
    f32 = lambda *shape: jax.ShapeDtypeStruct(shape, jnp.float32)
    smem = pl.BlockSpec(memory_space=pltpu.SMEM)
    vmem = pl.BlockSpec(memory_space=pltpu.VMEM)
    return pl.pallas_call(
        remap_kernel,
        out_shape=[f32(8, 6 * GROUP), f32(8, 10 * GROUP)]
        + [f32(8, n * HALF) for n in (1, 2, 2, 3)]
        + [f32(8, HALF)] * 10
        + [f32(8, 2 * HALF)] * 7,
        in_specs=[smem, smem, pl.BlockSpec(memory_space=pltpu.HBM), vmem],
        out_specs=[vmem] * 23,
        scratch_shapes=[
            pltpu.VMEM((LEV, PTS), jnp.float32),
            pltpu.SemaphoreType.DMA((16,)),
        ]
        + [pltpu.VMEM((CELLS, 128), jnp.float32)] * CHAINS
        + [pltpu.VMEM((BLK, 128), jnp.float32)] * (4 * CHAINS),
        compiler_params=pltpu.CompilerParams(vmem_limit_bytes=48 * 2**20),
    )(where, targets, trajectory, weights)


def fetch_kernel(sources, *refs):
    where_ref, t_ref, w_ref = refs[:3]
    pieces = refs[3 : 3 + len(sources)]
    out_hbm = refs[3 + len(sources)]
    rows, out, out_sem = refs[4 + len(sources) : 7 + len(sources)]
    turned = refs[7 + len(sources) :]
    core, z, y = where_ref[0], where_ref[1], where_ref[2]
    spans = [(part, to, width, piece, source) for piece, given in zip(pieces, sources)
             for part, source, width, to in given]
    for start, group, inside, width in (
        (0, 0, 0, GROUP),
        (GROUP, 1, 0, GROUP // 2),
        (HALF, 1, GROUP // 2, GROUP // 2),
        (HALF + GROUP // 2, 2, 0, GROUP),
        (3 * GROUP, 3, 0, GROUP),
    ):
        base = place(core, group) + inside
        found = {}
        for part, to, length, piece, source in spans:
            if to <= start and start + width <= to + length:
                found[part] = (piece, source + start - to)

        @pl.loop(0, width // 512)
        def _(i):
            for j in range(4):
                step = i * 512 + j * 128
                block = jnp.concatenate(
                    [
                        found[part][0][:, pl.ds(pl.multiple_of(found[part][1] + step, 128), 128)]
                        for part in range(16)
                    ],
                    axis=0,
                )
                rows[pl.ds(pl.multiple_of(base + step, 128), 128), :] = block.T

    share = PTS // 4
    stores = []
    for h in range(4):
        for q in range(share // BLK):
            at = h * share + q * BLK
            for u in range(BLK):
                cell = t_ref[at + u]
                turned[q][pl.ds(u, 1), :] = rows[pl.ds(cell, 1), :]
            out[:, pl.ds(at, BLK)] = turned[q][...].T * w_ref[:, pl.ds(at, BLK)]
        for part in range(16):
            store = pltpu.make_async_copy(
                out.at[pl.ds(part * 8, 8), pl.ds(h * share, share)],
                out_hbm.at[pl.ds(level_block(z, y, part), 8), pl.ds(h * share, share)],
                out_sem.at[h * 16 + part],
            )
            store.start()
            stores.append(store)
    for store in stores:
        store.wait()


def fetch(where, cells, weights, pieces, sources):
    smem = pl.BlockSpec(memory_space=pltpu.SMEM)
    vmem = pl.BlockSpec(memory_space=pltpu.VMEM)
    return pl.pallas_call(
        functools.partial(fetch_kernel, sources),
        out_shape=jax.ShapeDtypeStruct((LEV, PTS), jnp.float32),
        in_specs=[smem, smem] + [vmem] * (1 + len(pieces)),
        out_specs=pl.BlockSpec(memory_space=pl.ANY),
        scratch_shapes=[
            pltpu.VMEM((CELLS, 128), jnp.float32),
            pltpu.VMEM((LEV, PTS), jnp.float32),
            pltpu.SemaphoreType.DMA((64,)),
        ]
        + [pltpu.VMEM((BLK, 128), jnp.float32)] * 16,
        compiler_params=pltpu.CompilerParams(vmem_limit_bytes=40 * 2**20),
    )(where, cells, weights, *pieces)


def keep_columns(target, value):
    for c in range(target.shape[0]):
        target[c] = value[:, c * 128 : (c + 1) * 128]


def every(source, start, count, stride):
    return jnp.concatenate(
        [source[c, pl.ds(start, count, stride=stride), :] for c in range(source.shape[0])], axis=1
    )


def forward_kernel(own_ref, p_ref, m_ref, both_ref, y_ref, high_ref, low_ref, o_ref, work):
    b = own_ref[...] + p_ref[...] + m_ref[...]
    a = both_ref[:, :HALF] + y_ref[...]
    rows = [b[:, r * NLON : (r + 1) * NLON] for r in range(12)]
    rows += [a[:, r * NLON : (r + 1) * NLON] for r in range(12)]
    left = halves(jnp.concatenate(rows, axis=0))
    keep_columns(work, split_dot(left, (high_ref[...], low_ref[...])))
    for a in range(8):
        lines = every(work, a, 24, 8)
        for i in range(16):
            o_ref[i, :, a * 32 : (a + 1) * 32] = lines[:, i * 32 : (i + 1) * 32]


def forward(sums, high, low):
    return pl.pallas_call(
        forward_kernel,
        out_shape=jax.ShapeDtypeStruct((16, 24, 256), jnp.float32),
        scratch_shapes=[pltpu.VMEM((4, 192, 128), jnp.float32)],
        compiler_params=pltpu.CompilerParams(vmem_limit_bytes=16 * 2**20),
    )(*sums, high, low)


def legendre_kernel(first_ref, x_ref, high_ref, low_ref, coef_ref, o_ref, lines, back):
    bands = []
    for i in range(16):
        inner, outer = x_ref[i, 0:8], x_ref[i, 8:16]
        if i % 2 == 0:
            if i > 0:
                outer = outer + x_ref[i - 1, 16:24]
            bands += [outer, inner]
        else:
            if i < 15:
                outer = outer + x_ref[i + 1, 16:24]
            bands += [inner, outer]
    keep_columns(lines, jnp.concatenate(bands, axis=0).T)
    coef = jnp.concatenate([coef_ref[...]] * 2, axis=0)
    total = lax.broadcasted_iota(jnp.int32, (16, 256), 1)
    for m in range(16):
        left = jnp.concatenate(
            [every(lines, 2 * m, 8, 32), every(lines, 2 * m + 1, 8, 32)], axis=0
        )
        table = (high_ref[m], low_ref[m])
        spec = split_dot(halves(left), table)
        spec = jnp.where(total >= first_ref[0] + m, spec * coef, 0.0)
        result = split_dot(halves(spec), table, (((1,), (1,)), ((), ())))
        for c in range(2):
            part = result[:, c * 128 : (c + 1) * 128]
            back[c, pl.ds(2 * m, 8, stride=32), :] = part[:8]
            back[c, pl.ds(2 * m + 1, 8, stride=32), :] = part[8:]
    whole = jnp.concatenate([back[c].T for c in range(2)], axis=0)
    nothing = jnp.zeros((8, 256), jnp.float32)
    for i in range(16):
        low, top = whole[16 * i : 16 * i + 8], whole[16 * i + 8 : 16 * i + 16]
        if i % 2 == 0:
            rim = whole[16 * i - 8 : 16 * i] if i > 0 else nothing
            parts = [top, low, rim]
        else:
            rim = whole[16 * i + 16 : 16 * i + 24] if i < 15 else nothing
            parts = [low, top, rim]
        o_ref[i] = jnp.concatenate(parts, axis=0)


def spectral(first, x, table, coef):
    vmem = pl.BlockSpec(memory_space=pltpu.VMEM)
    return pl.pallas_call(
        legendre_kernel,
        out_shape=jax.ShapeDtypeStruct((16, 24, 256), jnp.float32),
        in_specs=[pl.BlockSpec(memory_space=pltpu.SMEM)] + [vmem] * 4,
        scratch_shapes=[pltpu.VMEM((2, 256, 128), jnp.float32)] * 2,
        compiler_params=pltpu.CompilerParams(vmem_limit_bytes=24 * 2**20),
    )(first, x, *table, coef)


def split_kernel(x_ref, high_ref, low_ref):
    @pl.loop(0, x_ref.shape[0])
    def _(m):
        high_ref[m], low_ref[m] = halves(x_ref[m])


def split_table(x):
    half = jax.ShapeDtypeStruct(x.shape, jnp.bfloat16)
    return pl.pallas_call(
        split_kernel,
        out_shape=[half, half],
        cost_estimate=pl.CostEstimate(
            flops=4 * x.size, bytes_accessed=8 * x.size, transcendentals=0
        ),
        compiler_params=pltpu.CompilerParams(vmem_limit_bytes=24 * 2**20),
    )(x)


def inverse_kernel(x_ref, high_ref, low_ref, a_ref, b_ref, work, lines):
    for a in range(8):
        for i in range(16):
            work[a * 24 : (a + 1) * 24, i * 32 : (i + 1) * 32] = x_ref[i, :, a * 32 : (a + 1) * 32]
    table = (high_ref[...], low_ref[...])
    keep_columns(lines, split_dot(halves(work[...]), table, (((1,), (1,)), ((), ()))))
    for r in range(24):
        out = a_ref if r < 12 else b_ref
        at = (r % 12) * NLON
        out[:, at : at + NLON] = every(lines, r, 8, 24)


def inverse(x, high, low):
    half = jax.ShapeDtypeStruct((8, HALF), jnp.float32)
    return pl.pallas_call(
        inverse_kernel,
        out_shape=[half, half],
        scratch_shapes=[pltpu.VMEM((192, 512), jnp.float32), pltpu.VMEM((4, 192, 128), jnp.float32)],
        compiler_params=pltpu.CompilerParams(vmem_limit_bytes=16 * 2**20),
    )(x, high, low)


ALONG = [(b, (b + 2) % 16) for b in range(16)]
AGAINST = [(b, (b - 2) % 16) for b in range(16)]
ACROSS = [(b, b ^ 1) for b in range(16)]


def ahead(x):
    return lax.ppermute(x, "bulk", ALONG)


def behind(x):
    return lax.ppermute(x, "bulk", AGAINST)


def across(x):
    return lax.ppermute(x, "bulk", ACROSS)


def other_core(x):
    return lax.ppermute(x, "inner", ACROSS)


def loosely(*moves, free=(), late=()):
    results = [move(value) for move, value in list(moves) + list(free)]
    held = lax.optimization_barrier(tuple(results[: len(moves)]) + tuple(late))
    return held[: len(moves)], results[len(moves) :], held[len(moves) :]


def together(*moves, free=(), late=()):
    both = list(moves) + list(free)
    values = lax.optimization_barrier(tuple(value for _, value in both))
    both = [(move, value) for (move, _), value in zip(both, values)]
    return loosely(*both[: len(moves)], free=both[len(moves) :], late=late)


def wide(*blocks):
    return jnp.concatenate(blocks, axis=1)


def gather_sums(legendre, targets, cross_far, cross, y1, y2, y3, y4, *rest):
    keep, far_p, far_m = rest[:8], rest[8], rest[9]
    flat = lambda k: rest[10 + NEAR.index(k)]
    quarter = HALF // 2

    def with_core(piece, add):
        return wide(piece[:, :GROUP] + add, piece[:, GROUP:])

    def part_of(source, n, width):
        return source[:, n * width : (n + 1) * width]

    (shared_far,), (p, m), _ = loosely(
        (other_core, cross_far), free=[(ahead, far_p), (behind, far_m)]
    )

    def from_core(k, r):
        source, parts = (shared_far, FAR) if k in (3, 4, 5) else (shared, REST)
        return part_of(source, parts.index(2 * k + r), GROUP)

    mine = lambda k: with_core(keep[k], from_core(k, 0))
    send = lambda piece, *order: wide(
        *[with_core(part_of(piece, i, HALF), from_core(k, 1)) for i, k in enumerate(order)]
    )
    (y, shared), _, (p, m) = loosely(
        (across, send(y1, 4)), (other_core, cross), late=[p, m]
    )
    here = mine(4) + y
    at_home = with_core(part_of(y4, 2, HALF), from_core(0, 1))
    (p, y), (m,), _ = loosely(
        (ahead, wide(flat(3) + wide(p, jnp.zeros_like(p)), here[:, :quarter])),
        (across, wide(send(y2, 3, 5), at_home[:, :quarter])),
        free=[(behind, wide(flat(5) + wide(jnp.zeros_like(m), m), here[:, quarter:]))],
    )
    here_p = mine(3) + y[:, :HALF]
    here_m = mine(5) + y[:, HALF : 2 * HALF]
    here_p = wide(here_p[:, :quarter] + p[:, 2 * HALF :], here_p[:, quarter:])
    here_m = wide(here_m[:, :quarter], here_m[:, quarter:] + m[:, 2 * HALF :])
    home = y[:, 2 * HALF :]
    (p, y, cells), (m,), _ = loosely(
        (ahead, wide(flat(2) + p[:, : 2 * HALF], here_p)),
        (across, wide(send(y3, 2, 6), at_home[:, quarter:])),
        (lambda t: t & (CELLS - 1), targets),
        free=[(behind, wide(flat(6) + m[:, : 2 * HALF], here_m))],
    )
    own = mine(0) + wide(home, y[:, 2 * HALF :])
    (p, y), (m,), _ = loosely(
        (ahead, wide(flat(1), mine(2) + y[:, :HALF]) + p),
        (across, send(y4, 1, 7)),
        free=[(behind, wide(flat(7), mine(6) + y[:, HALF : 2 * HALF]) + m)],
    )
    both = flat(0) + p[:, : 2 * HALF] + m[:, : 2 * HALF]
    p, m, y, table = loosely(
        (ahead, mine(1) + y[:, :HALF] + p[:, 2 * HALF :]),
        (behind, mine(7) + y[:, HALF:] + m[:, 2 * HALF :]),
        (across, both[:, HALF:]),
        (split_table, legendre),
    )[0]
    return (own, p, m, both, y), table, cells


def spread_field(a, b):
    pieces, sources = [], []
    quarter = HALF // 2

    def give(piece, *spans):
        pieces.append(piece)
        sources.append(spans)

    def first(k, r, source):
        return (2 * k + r, source, HALF, 0)

    def second(k, r, source):
        return (2 * k + r, source, HALF, HALF)

    def all_of(k, source):
        return [second(k, 0, source), second(k, 1, source + HALF)]

    def heads(*given):
        value = wide(*[array[:, at : at + GROUP] for _, array, at in given])
        return value, [(part, n * GROUP, GROUP, 3 * GROUP) for n, (part, _, _) in enumerate(given)]

    give(a, first(0, 0, 0))
    give(b, second(0, 0, 0))
    (p1, m1, y0), _, _ = together((ahead, a), (behind, a), (across, b))
    give(y0, second(0, 1, 0))
    give(p1, first(7, 0, 0))
    give(m1, first(1, 0, 0))
    pair = wide(b, y0)
    (p, m), (y1,), _ = together(
        (ahead, wide(pair, p1)),
        (behind, wide(pair, m1)),
        free=[(across, wide(a, p1, m1))],
    )
    give(p, *all_of(7, 0), first(6, 0, 2 * HALF))
    give(m, *all_of(1, 0), first(2, 0, 2 * HALF))
    core1, spans1 = heads(
        (0, a, 0), (14, p1, 0), (2, m1, 0), (12, p, 2 * HALF), (4, m, 2 * HALF)
    )
    (p, m, y2), (core1,), (y1,) = together(
        (ahead, p),
        (behind, m),
        (across, wide(p[:, 2 * HALF :], m[:, 2 * HALF :])),
        free=[(other_core, core1)],
        late=[y1],
    )
    give(y1, first(0, 1, 0), first(7, 1, HALF), first(1, 1, 2 * HALF))
    give(p, *all_of(6, 0), first(5, 0, 2 * HALF))
    give(m, *all_of(2, 0), first(3, 0, 2 * HALF))
    core2, spans2 = heads(
        (1, y1, 0), (15, y1, HALF), (3, y1, 2 * HALF), (10, p, 2 * HALF), (6, m, 2 * HALF)
    )
    (p, m, y3), (core2,), (core1,) = together(
        (ahead, p[:, : 2 * HALF + quarter]),
        (behind, wide(m[:, : 2 * HALF], m[:, 2 * HALF + quarter :])),
        (across, wide(p[:, 2 * HALF :], m[:, 2 * HALF :])),
        free=[(other_core, core2)],
        late=[core1],
    )
    give(core1, *spans1)
    give(y2, first(6, 1, 0), first(2, 1, HALF))
    give(p, *all_of(5, 0))
    give(m, *all_of(3, 0))
    far = wide(p[:, 2 * HALF :], m[:, 2 * HALF :])
    give(far, first(4, 0, 0))
    core3, spans3 = heads((13, y2, 0), (5, y2, HALF), (8, far, 0))
    (p, m, y4), (core3,), (core2,) = together(
        (ahead, p[:, :HALF]),
        (behind, m[:, HALF : 2 * HALF]),
        (across, far),
        free=[(other_core, core3)],
        late=[core2],
    )
    give(core2, *spans2)
    give(y3, first(5, 1, 0), first(3, 1, HALF))
    give(p, second(4, 0, 0))
    give(m, second(4, 1, 0))
    give(y4, first(4, 1, 0))
    core4, spans4 = heads((11, y3, 0), (7, y3, HALF), (9, y4, 0))
    (core4,), _, (core3,) = together((other_core, core4), late=[core3])
    give(core3, *spans3)
    give(core4, *spans4)
    return pieces, sources


def shards(trajectory, targets, remap_weights, legendre, spectral_coef):
    inner = lax.axis_index("inner")
    bulk = lax.axis_index("bulk")
    where = jnp.stack([inner % 2, bulk // 2, bulk % 2]).astype(jnp.int32)
    weights = remap_weights[None, :]
    high, low = (jnp.asarray(t) for t in tables())
    sums, table, cells = gather_sums(legendre, targets, *remap(where, targets, trajectory, weights))
    sent = lax.all_to_all(forward(sums, high, low), "inner", 0, 0, tiled=True)
    first = (inner * 16).astype(jnp.int32)[None]
    back = spectral(first, sent, table, spectral_coef)
    back = lax.all_to_all(back, "inner", 0, 0, tiled=True)
    pieces, sources = spread_field(*inverse(back, high, low))
    return fetch(where, cells, weights, pieces, sources)


def solution(mesh):
    placed = (
        P(None, ("inner", "bulk")),
        P(("inner", "bulk")),
        P(("inner", "bulk")),
        P("inner", None, None),
        P("bulk", None),
    )
    return jax.shard_map(
        shards, mesh=mesh, in_specs=placed, out_specs=P(None, ("inner", "bulk")), check_vma=False
    )
```

```python
import functools

import jax
import jax.numpy as jnp
import ml_dtypes
import numpy as np
from jax import lax
from jax.experimental import pallas as pl
from jax.experimental.pallas import tpu as pltpu
from jax.sharding import PartitionSpec as P

NLAT = 256
NLON = 512
M = 256
LEV = 128
PTS = 8192
GROUP = 8 * NLON
CELLS = 4 * GROUP
HALF = 3 * GROUP // 2
CHAINS = 4
BLK = 128
NEAR = (0, 1, 2, 3, 5, 6, 7)
FAR = tuple(2 * k + r for k in (4, 3, 5) for r in (0, 1))
REST = tuple(2 * k + r for k in (2, 6, 1, 7, 0) for r in (0, 1))

EVEN = (1, 0, 3, 2)
ODD = (2, 3, 0, 1)


def tables():
    wave = np.arange(M)
    lon = np.arange(NLON)
    angle = 2.0 * np.pi * ((wave[None, :] * lon[:, None]) % NLON) / NLON
    both = np.stack([np.cos(angle), -np.sin(angle)], axis=-1) / np.sqrt(NLON)
    full = both.reshape(NLON, 2 * M).astype(np.float32)
    high = full.astype(ml_dtypes.bfloat16)
    low = (full - high.astype(np.float32)).astype(ml_dtypes.bfloat16)
    return high, low


def halves(value):
    high = value.astype(jnp.bfloat16)
    low = (value - high.astype(jnp.float32)).astype(jnp.bfloat16)
    return high, low


def split_dot(left, right, dims=(((1,), (0,)), ((), ()))):
    dot = functools.partial(
        lax.dot_general, dimension_numbers=dims, preferred_element_type=jnp.float32
    )
    rows = left[0].shape[0]
    both = dot(jnp.concatenate(left, axis=0), right[0])
    return both[:rows] + (dot(left[0], right[1]) + both[rows:])


def place(core, group):
    return pl.multiple_of(jnp.where(core == 0, EVEN[group], ODD[group]) * GROUP, GROUP)


def level_block(z, y, part):
    row = lax.rem(z + part // 2, 8) * 2 + lax.rem(y + part % 2, 2)
    return pl.multiple_of(row * 8, 8)


def remap_kernel(
    where_ref, t_ref, x_hbm, w_ref,
    *refs,
):
    outs, (x_ref, in_sem, *work) = refs[:24], refs[24:]
    totals, turned = work[:CHAINS], work[CHAINS:]
    core, z, y = where_ref[0], where_ref[1], where_ref[2]
    loads = []
    for part in range(16):
        load = pltpu.make_async_copy(
            x_hbm.at[pl.ds(level_block(z, y, part), 8), :],
            x_ref.at[pl.ds(part * 8, 8), :],
            in_sem.at[part],
        )
        load.start()
        loads.append(load)
    zero = jnp.zeros((256, 128), jnp.float32)

    @pl.loop(0, CELLS // 256)
    def _(i):
        for total in totals:
            total[pl.ds(i * 256, 256), :] = zero

    for load in loads:
        load.wait()
    share = PTS // CHAINS

    @pl.loop(0, share // (4 * BLK))
    def _(b):
        for n in range(4):
            for q in range(CHAINS):
                at = pl.multiple_of(q * share + (4 * b + n) * BLK, BLK)
                turned[4 * q + n][...] = (x_ref[:, pl.ds(at, BLK)] * w_ref[:, pl.ds(at, BLK)]).T
            for u in range(BLK):
                for q in range(CHAINS):
                    cell = t_ref[q * share + (4 * b + n) * BLK + u] & (CELLS - 1)
                    totals[q][pl.ds(cell, 1), :] += turned[4 * q + n][pl.ds(u, 1), :]

    def summed(start):
        value = totals[0][pl.ds(start, 128), :] + totals[1][pl.ds(start, 128), :]
        other = totals[2][pl.ds(start, 128), :] + totals[3][pl.ds(start, 128), :]
        return (value + other).T

    def fill(targets, group, source, count, to):
        base = place(core, group) + source

        @pl.loop(0, count // 512)
        def _(i):
            for j in range(4):
                step = i * 512 + j * 128
                block = summed(pl.multiple_of(base + step, 128))
                for part, (target, start) in targets.items():
                    at = pl.multiple_of(start + to + step, 128)
                    target[:, pl.ds(at, 128)] = block[part * 8 : part * 8 + 8]

    outs = iter(outs)

    def take(width, *lists):
        found = {}
        for parts in lists:
            target = next(outs)
            found.update({part: (target, n * width) for n, part in enumerate(parts)})
        return found

    third = take(GROUP, FAR, REST)
    second = take(HALF, (9,), (7, 11), (5, 13), (3, 15), (1,), *[(2 * k,) for k in range(8)])
    first = take(HALF, (8,), (9,), *[(2 * k, 2 * k + 1) for k in NEAR])
    fill(third, 3, 0, GROUP, 0)
    fill(second, 0, 0, GROUP, 0)
    fill(second, 1, 0, GROUP // 2, GROUP)
    fill(first, 1, GROUP // 2, GROUP // 2, 0)
    fill(first, 2, 0, GROUP, GROUP // 2)


def remap(where, targets, trajectory, weights):
    f32 = lambda *shape: jax.ShapeDtypeStruct(shape, jnp.float32)
    smem = pl.BlockSpec(memory_space=pltpu.SMEM)
    vmem = pl.BlockSpec(memory_space=pltpu.VMEM)
    return pl.pallas_call(
        remap_kernel,
        out_shape=[f32(8, 6 * GROUP), f32(8, 10 * GROUP)]
        + [f32(8, n * HALF) for n in (1, 2, 2, 2, 1)]
        + [f32(8, HALF)] * 10
        + [f32(8, 2 * HALF)] * 7,
        in_specs=[smem, smem, pl.BlockSpec(memory_space=pltpu.HBM), vmem],
        out_specs=[vmem] * 24,
        scratch_shapes=[
            pltpu.VMEM((LEV, PTS), jnp.float32),
            pltpu.SemaphoreType.DMA((16,)),
        ]
        + [pltpu.VMEM((CELLS, 128), jnp.float32)] * CHAINS
        + [pltpu.VMEM((BLK, 128), jnp.float32)] * (4 * CHAINS),
        compiler_params=pltpu.CompilerParams(vmem_limit_bytes=48 * 2**20),
    )(where, targets, trajectory, weights)


def fetch_kernel(sources, *refs):
    where_ref, t_ref, w_ref = refs[:3]
    pieces = refs[3 : 3 + len(sources)]
    out_hbm = refs[3 + len(sources)]
    rows, out, out_sem = refs[4 + len(sources) : 7 + len(sources)]
    turned = refs[7 + len(sources) :]
    core, z, y = where_ref[0], where_ref[1], where_ref[2]
    spans = [(part, to, width, piece, source) for piece, given in zip(pieces, sources)
             for part, source, width, to in given]
    for start, group, inside, width in (
        (0, 0, 0, GROUP),
        (GROUP, 1, 0, GROUP // 2),
        (HALF, 1, GROUP // 2, GROUP // 2),
        (HALF + GROUP // 2, 2, 0, GROUP),
        (3 * GROUP, 3, 0, GROUP),
    ):
        base = place(core, group) + inside
        found = {}
        for part, to, length, piece, source in spans:
            if to <= start and start + width <= to + length:
                found[part] = (piece, source + start - to)

        @pl.loop(0, width // 512)
        def _(i):
            for j in range(4):
                step = i * 512 + j * 128
                block = jnp.concatenate(
                    [
                        found[part][0][:, pl.ds(pl.multiple_of(found[part][1] + step, 128), 128)]
                        for part in range(16)
                    ],
                    axis=0,
                )
                rows[pl.ds(pl.multiple_of(base + step, 128), 128), :] = block.T

    share = PTS // 4
    stores = []
    for h in range(4):
        for q in range(share // BLK):
            at = h * share + q * BLK
            for u in range(BLK):
                cell = t_ref[at + u]
                turned[q][pl.ds(u, 1), :] = rows[pl.ds(cell, 1), :]
            out[:, pl.ds(at, BLK)] = turned[q][...].T * w_ref[:, pl.ds(at, BLK)]
        for part in range(16):
            store = pltpu.make_async_copy(
                out.at[pl.ds(part * 8, 8), pl.ds(h * share, share)],
                out_hbm.at[pl.ds(level_block(z, y, part), 8), pl.ds(h * share, share)],
                out_sem.at[h * 16 + part],
            )
            store.start()
            stores.append(store)
    for store in stores:
        store.wait()


def fetch(where, cells, weights, pieces, sources):
    smem = pl.BlockSpec(memory_space=pltpu.SMEM)
    vmem = pl.BlockSpec(memory_space=pltpu.VMEM)
    return pl.pallas_call(
        functools.partial(fetch_kernel, sources),
        out_shape=jax.ShapeDtypeStruct((LEV, PTS), jnp.float32),
        in_specs=[smem, smem] + [vmem] * (1 + len(pieces)),
        out_specs=pl.BlockSpec(memory_space=pl.ANY),
        scratch_shapes=[
            pltpu.VMEM((CELLS, 128), jnp.float32),
            pltpu.VMEM((LEV, PTS), jnp.float32),
            pltpu.SemaphoreType.DMA((64,)),
        ]
        + [pltpu.VMEM((BLK, 128), jnp.float32)] * 16,
        compiler_params=pltpu.CompilerParams(vmem_limit_bytes=40 * 2**20),
    )(where, cells, weights, *pieces)


def keep_columns(target, value):
    for c in range(target.shape[0]):
        target[c] = value[:, c * 128 : (c + 1) * 128]


def every(source, start, count, stride):
    return jnp.concatenate(
        [source[c, pl.ds(start, count, stride=stride), :] for c in range(source.shape[0])], axis=1
    )


def forward_kernel(own_ref, p_ref, m_ref, both_ref, y_ref, high_ref, low_ref, o_ref, work):
    b = own_ref[...] + p_ref[...] + m_ref[...]
    a = both_ref[:, :HALF] + y_ref[...]
    rows = [b[:, r * NLON : (r + 1) * NLON] for r in range(12)]
    rows += [a[:, r * NLON : (r + 1) * NLON] for r in range(12)]
    left = halves(jnp.concatenate(rows, axis=0))
    keep_columns(work, split_dot(left, (high_ref[...], low_ref[...])))
    for a in range(8):
        lines = every(work, a, 24, 8)
        for i in range(16):
            o_ref[i, :, a * 32 : (a + 1) * 32] = lines[:, i * 32 : (i + 1) * 32]


def forward(sums, high, low):
    return pl.pallas_call(
        forward_kernel,
        out_shape=jax.ShapeDtypeStruct((16, 24, 256), jnp.float32),
        scratch_shapes=[pltpu.VMEM((4, 192, 128), jnp.float32)],
        compiler_params=pltpu.CompilerParams(vmem_limit_bytes=16 * 2**20),
    )(*sums, high, low)


def legendre_kernel(first_ref, x_ref, high_ref, low_ref, coef_ref, o_ref, lines, back):
    bands = []
    for i in range(16):
        inner, outer = x_ref[i, 0:8], x_ref[i, 8:16]
        if i % 2 == 0:
            if i > 0:
                outer = outer + x_ref[i - 1, 16:24]
            bands += [outer, inner]
        else:
            if i < 15:
                outer = outer + x_ref[i + 1, 16:24]
            bands += [inner, outer]
    keep_columns(lines, jnp.concatenate(bands, axis=0).T)
    coef = jnp.concatenate([coef_ref[...]] * 2, axis=0)
    total = lax.broadcasted_iota(jnp.int32, (16, 256), 1)
    for m in range(16):
        left = jnp.concatenate(
            [every(lines, 2 * m, 8, 32), every(lines, 2 * m + 1, 8, 32)], axis=0
        )
        table = (high_ref[m], low_ref[m])
        spec = split_dot(halves(left), table)
        spec = jnp.where(total >= first_ref[0] + m, spec * coef, 0.0)
        result = split_dot(halves(spec), table, (((1,), (1,)), ((), ())))
        for c in range(2):
            part = result[:, c * 128 : (c + 1) * 128]
            back[c, pl.ds(2 * m, 8, stride=32), :] = part[:8]
            back[c, pl.ds(2 * m + 1, 8, stride=32), :] = part[8:]
    whole = jnp.concatenate([back[c].T for c in range(2)], axis=0)
    nothing = jnp.zeros((8, 256), jnp.float32)
    for i in range(16):
        low, top = whole[16 * i : 16 * i + 8], whole[16 * i + 8 : 16 * i + 16]
        if i % 2 == 0:
            rim = whole[16 * i - 8 : 16 * i] if i > 0 else nothing
            parts = [top, low, rim]
        else:
            rim = whole[16 * i + 16 : 16 * i + 24] if i < 15 else nothing
            parts = [low, top, rim]
        o_ref[i] = jnp.concatenate(parts, axis=0)


def spectral(first, x, table, coef):
    vmem = pl.BlockSpec(memory_space=pltpu.VMEM)
    return pl.pallas_call(
        legendre_kernel,
        out_shape=jax.ShapeDtypeStruct((16, 24, 256), jnp.float32),
        in_specs=[pl.BlockSpec(memory_space=pltpu.SMEM)] + [vmem] * 4,
        scratch_shapes=[pltpu.VMEM((2, 256, 128), jnp.float32)] * 2,
        compiler_params=pltpu.CompilerParams(vmem_limit_bytes=24 * 2**20),
    )(first, x, *table, coef)


def split_kernel(x_ref, high_ref, low_ref):
    @pl.loop(0, x_ref.shape[0])
    def _(m):
        high_ref[m], low_ref[m] = halves(x_ref[m])


def split_table(x):
    half = jax.ShapeDtypeStruct(x.shape, jnp.bfloat16)
    return pl.pallas_call(
        split_kernel,
        out_shape=[half, half],
        cost_estimate=pl.CostEstimate(
            flops=4 * x.size, bytes_accessed=8 * x.size, transcendentals=0
        ),
        compiler_params=pltpu.CompilerParams(vmem_limit_bytes=24 * 2**20),
    )(x)


def inverse_kernel(x_ref, high_ref, low_ref, a_ref, b_ref, work, lines):
    for a in range(8):
        for i in range(16):
            work[a * 24 : (a + 1) * 24, i * 32 : (i + 1) * 32] = x_ref[i, :, a * 32 : (a + 1) * 32]
    table = (high_ref[...], low_ref[...])
    keep_columns(lines, split_dot(halves(work[...]), table, (((1,), (1,)), ((), ()))))
    for r in range(24):
        out = a_ref if r < 12 else b_ref
        at = (r % 12) * NLON
        out[:, at : at + NLON] = every(lines, r, 8, 24)


def inverse(x, high, low):
    half = jax.ShapeDtypeStruct((8, HALF), jnp.float32)
    return pl.pallas_call(
        inverse_kernel,
        out_shape=[half, half],
        scratch_shapes=[pltpu.VMEM((192, 512), jnp.float32), pltpu.VMEM((4, 192, 128), jnp.float32)],
        compiler_params=pltpu.CompilerParams(vmem_limit_bytes=16 * 2**20),
    )(x, high, low)


ALONG = [(b, (b + 2) % 16) for b in range(16)]
AGAINST = [(b, (b - 2) % 16) for b in range(16)]
ACROSS = [(b, b ^ 1) for b in range(16)]


def ahead(x):
    return lax.ppermute(x, "bulk", ALONG)


def behind(x):
    return lax.ppermute(x, "bulk", AGAINST)


def across(x):
    return lax.ppermute(x, "bulk", ACROSS)


def other_core(x):
    return lax.ppermute(x, "inner", ACROSS)


def loosely(*moves, free=(), late=()):
    results = [move(value) for move, value in list(moves) + list(free)]
    held = lax.optimization_barrier(tuple(results[: len(moves)]) + tuple(late))
    return held[: len(moves)], results[len(moves) :], held[len(moves) :]


def together(*moves, free=(), late=()):
    both = list(moves) + list(free)
    values = lax.optimization_barrier(tuple(value for _, value in both))
    both = [(move, value) for (move, _), value in zip(both, values)]
    return loosely(*both[: len(moves)], free=both[len(moves) :], late=late)


def wide(*blocks):
    return jnp.concatenate(blocks, axis=1)


def gather_sums(legendre, targets, cross_far, cross, y1, y2, y3, y4, y5, *rest):
    keep, far_p, far_m = rest[:8], rest[8], rest[9]
    flat = lambda k: rest[10 + NEAR.index(k)]
    quarter = HALF // 2

    def with_core(piece, add):
        return wide(piece[:, :GROUP] + add, piece[:, GROUP:])

    def part_of(source, n, width):
        return source[:, n * width : (n + 1) * width]

    (shared_far,), (p, m), _ = loosely(
        (other_core, cross_far), free=[(ahead, far_p), (behind, far_m)]
    )

    def from_core(k, r):
        source, parts = (shared_far, FAR) if k in (3, 4, 5) else (shared, REST)
        return part_of(source, parts.index(2 * k + r), GROUP)

    mine = lambda k: with_core(keep[k], from_core(k, 0))
    send = lambda piece, *order: wide(
        *[with_core(part_of(piece, i, HALF), from_core(k, 1)) for i, k in enumerate(order)]
    )
    (y, shared), _, (p, m) = loosely(
        (across, send(y1, 4)), (other_core, cross), late=[p, m]
    )
    here = mine(4) + y
    at_home = with_core(y5, from_core(0, 1))
    (p, y), (m,), _ = loosely(
        (ahead, wide(flat(3) + wide(p, jnp.zeros_like(p)), here[:, :quarter])),
        (across, wide(send(y2, 3, 5), at_home[:, :quarter])),
        free=[(behind, wide(flat(5) + wide(jnp.zeros_like(m), m), here[:, quarter:]))],
    )
    here_p = mine(3) + y[:, :HALF]
    here_m = mine(5) + y[:, HALF : 2 * HALF]
    here_p = wide(here_p[:, :quarter] + p[:, 2 * HALF :], here_p[:, quarter:])
    here_m = wide(here_m[:, :quarter], here_m[:, quarter:] + m[:, 2 * HALF :])
    home = y[:, 2 * HALF :]
    held_targets, y = lax.optimization_barrier((targets, y))
    (p, y, cells), (m,), _ = loosely(
        (ahead, wide(flat(2) + p[:, : 2 * HALF], here_p)),
        (across, wide(send(y3, 2, 6), at_home[:, quarter:])),
        (lambda t: t & (CELLS - 1), held_targets),
        free=[(behind, wide(flat(6) + m[:, : 2 * HALF], here_m))],
    )
    own = mine(0) + wide(home, y[:, 2 * HALF :])
    (p, y), (m,), _ = loosely(
        (ahead, wide(flat(1), mine(2) + y[:, :HALF]) + p),
        (across, send(y4, 1, 7)),
        free=[(behind, wide(flat(7), mine(6) + y[:, HALF : 2 * HALF]) + m)],
    )
    both = flat(0) + p[:, : 2 * HALF] + m[:, : 2 * HALF]
    p, m, y, table = loosely(
        (ahead, mine(1) + y[:, :HALF] + p[:, 2 * HALF :]),
        (behind, mine(7) + y[:, HALF:] + m[:, 2 * HALF :]),
        (across, both[:, HALF:]),
        (split_table, legendre),
    )[0]
    return (own, p, m, both, y), table, cells


def spread_field(a, b):
    pieces, sources = [], []
    quarter = HALF // 2

    def give(piece, *spans):
        pieces.append(piece)
        sources.append(spans)

    def first(k, r, source):
        return (2 * k + r, source, HALF, 0)

    def second(k, r, source):
        return (2 * k + r, source, HALF, HALF)

    def all_of(k, source):
        return [second(k, 0, source), second(k, 1, source + HALF)]

    def heads(*given):
        value = wide(*[array[:, at : at + GROUP] for _, array, at in given])
        return value, [(part, n * GROUP, GROUP, 3 * GROUP) for n, (part, _, _) in enumerate(given)]

    give(a, first(0, 0, 0))
    give(b, second(0, 0, 0))
    (p1, m1, y0), _, _ = together((ahead, a), (behind, a), (across, b))
    give(y0, second(0, 1, 0))
    give(p1, first(7, 0, 0))
    give(m1, first(1, 0, 0))
    pair = wide(b, y0)
    (p, m), (y1,), _ = together(
        (ahead, wide(pair, p1)),
        (behind, wide(pair, m1)),
        free=[(across, wide(a, p1, m1))],
    )
    give(p, *all_of(7, 0), first(6, 0, 2 * HALF))
    give(m, *all_of(1, 0), first(2, 0, 2 * HALF))
    core1, spans1 = heads(
        (0, a, 0), (14, p1, 0), (2, m1, 0), (12, p, 2 * HALF), (4, m, 2 * HALF)
    )
    (p, m, y2), (core1,), (y1,) = together(
        (ahead, p),
        (behind, m),
        (across, wide(p[:, 2 * HALF :], m[:, 2 * HALF :])),
        free=[(other_core, core1)],
        late=[y1],
    )
    give(y1, first(0, 1, 0), first(7, 1, HALF), first(1, 1, 2 * HALF))
    give(p, *all_of(6, 0), first(5, 0, 2 * HALF))
    give(m, *all_of(2, 0), first(3, 0, 2 * HALF))
    core2, spans2 = heads(
        (1, y1, 0), (15, y1, HALF), (3, y1, 2 * HALF), (10, p, 2 * HALF), (6, m, 2 * HALF)
    )
    (p, m, y3), (core2,), (core1,) = together(
        (ahead, p[:, : 2 * HALF + quarter]),
        (behind, wide(m[:, : 2 * HALF], m[:, 2 * HALF + quarter :])),
        (across, wide(p[:, 2 * HALF :], m[:, 2 * HALF :])),
        free=[(other_core, core2)],
        late=[core1],
    )
    give(core1, *spans1)
    give(y2, first(6, 1, 0), first(2, 1, HALF))
    give(p, *all_of(5, 0))
    give(m, *all_of(3, 0))
    far = wide(p[:, 2 * HALF :], m[:, 2 * HALF :])
    give(far, first(4, 0, 0))
    core3, spans3 = heads((13, y2, 0), (5, y2, HALF), (8, far, 0))
    (p, m, y4), (core3,), (core2,) = together(
        (ahead, p[:, :HALF]),
        (behind, m[:, HALF : 2 * HALF]),
        (across, far),
        free=[(other_core, core3)],
        late=[core2],
    )
    give(core2, *spans2)
    give(y3, first(5, 1, 0), first(3, 1, HALF))
    give(p, second(4, 0, 0))
    give(m, second(4, 1, 0))
    give(y4, first(4, 1, 0))
    core4, spans4 = heads((11, y3, 0), (7, y3, HALF), (9, y4, 0))
    (core4,), _, (core3,) = together((other_core, core4), late=[core3])
    give(core3, *spans3)
    give(core4, *spans4)
    return pieces, sources


def shards(trajectory, targets, remap_weights, legendre, spectral_coef):
    inner = lax.axis_index("inner")
    bulk = lax.axis_index("bulk")
    where = jnp.stack([inner % 2, bulk // 2, bulk % 2]).astype(jnp.int32)
    weights = remap_weights[None, :]
    high, low = (jnp.asarray(t) for t in tables())
    sums, table, cells = gather_sums(legendre, targets, *remap(where, targets, trajectory, weights))
    sent = lax.all_to_all(forward(sums, high, low), "inner", 0, 0, tiled=True)
    first = (inner * 16).astype(jnp.int32)[None]
    back = spectral(first, sent, table, spectral_coef)
    back = lax.all_to_all(back, "inner", 0, 0, tiled=True)
    pieces, sources = spread_field(*inverse(back, high, low))
    return fetch(where, cells, weights, pieces, sources)


def solution(mesh):
    placed = (
        P(None, ("inner", "bulk")),
        P(("inner", "bulk")),
        P(("inner", "bulk")),
        P("inner", None, None),
        P("bulk", None),
    )
    return jax.shard_map(
        shards, mesh=mesh, in_specs=placed, out_specs=P(None, ("inner", "bulk")), check_vma=False
    )
```

```python
import functools

import jax
import jax.numpy as jnp
import ml_dtypes
import numpy as np
from jax import lax
from jax.experimental import pallas as pl
from jax.experimental.pallas import tpu as pltpu
from jax.sharding import PartitionSpec as P

NLAT = 256
NLON = 512
M = 256
LEV = 128
PTS = 8192
GROUP = 8 * NLON
CELLS = 4 * GROUP
HALF = 3 * GROUP // 2
CHAINS = 4
BLK = 128
NEAR = (0, 1, 2, 3, 5, 6, 7)
FAR = tuple(2 * k + r for k in (4, 3, 5) for r in (0, 1))
REST = tuple(2 * k + r for k in (2, 6, 1, 7, 0) for r in (0, 1))

EVEN = (1, 0, 3, 2)
ODD = (2, 3, 0, 1)


def tables():
    wave = np.arange(M)
    lon = np.arange(NLON)
    angle = 2.0 * np.pi * ((wave[None, :] * lon[:, None]) % NLON) / NLON
    both = np.stack([np.cos(angle), -np.sin(angle)], axis=-1) / np.sqrt(NLON)
    full = both.reshape(NLON, 2 * M).astype(np.float32)
    high = full.astype(ml_dtypes.bfloat16)
    low = (full - high.astype(np.float32)).astype(ml_dtypes.bfloat16)
    return high, low


def halves(value):
    high = value.astype(jnp.bfloat16)
    low = (value - high.astype(jnp.float32)).astype(jnp.bfloat16)
    return high, low


def split_dot(left, right, dims=(((1,), (0,)), ((), ()))):
    dot = functools.partial(
        lax.dot_general, dimension_numbers=dims, preferred_element_type=jnp.float32
    )
    rows = left[0].shape[0]
    both = dot(jnp.concatenate(left, axis=0), right[0])
    return both[:rows] + (dot(left[0], right[1]) + both[rows:])


def place(core, group):
    return pl.multiple_of(jnp.where(core == 0, EVEN[group], ODD[group]) * GROUP, GROUP)


def level_block(z, y, part):
    row = lax.rem(z + part // 2, 8) * 2 + lax.rem(y + part % 2, 2)
    return pl.multiple_of(row * 8, 8)


def remap_kernel(
    where_ref, t_ref, x_hbm, w_ref,
    *refs,
):
    outs, (x_ref, in_sem, *work) = refs[:24], refs[24:]
    totals, turned = work[:CHAINS], work[CHAINS:]
    core, z, y = where_ref[0], where_ref[1], where_ref[2]
    loads = []
    for part in range(16):
        load = pltpu.make_async_copy(
            x_hbm.at[pl.ds(level_block(z, y, part), 8), :],
            x_ref.at[pl.ds(part * 8, 8), :],
            in_sem.at[part],
        )
        load.start()
        loads.append(load)
    zero = jnp.zeros((256, 128), jnp.float32)

    @pl.loop(0, CELLS // 256)
    def _(i):
        for total in totals:
            total[pl.ds(i * 256, 256), :] = zero

    for load in loads:
        load.wait()
    share = PTS // CHAINS

    @pl.loop(0, share // (4 * BLK))
    def _(b):
        for n in range(4):
            for q in range(CHAINS):
                at = pl.multiple_of(q * share + (4 * b + n) * BLK, BLK)
                turned[4 * q + n][...] = (x_ref[:, pl.ds(at, BLK)] * w_ref[:, pl.ds(at, BLK)]).T
            for u in range(BLK):
                for q in range(CHAINS):
                    cell = t_ref[q * share + (4 * b + n) * BLK + u] & (CELLS - 1)
                    totals[q][pl.ds(cell, 1), :] += turned[4 * q + n][pl.ds(u, 1), :]

    def summed(start):
        value = totals[0][pl.ds(start, 128), :] + totals[1][pl.ds(start, 128), :]
        other = totals[2][pl.ds(start, 128), :] + totals[3][pl.ds(start, 128), :]
        return (value + other).T

    def fill(targets, group, source, count, to):
        base = place(core, group) + source

        @pl.loop(0, count // 2048)
        def _(i):
            for j in range(16):
                step = i * 2048 + j * 128
                block = summed(pl.multiple_of(base + step, 128))
                for part, (target, start) in targets.items():
                    at = pl.multiple_of(start + to + step, 128)
                    target[:, pl.ds(at, 128)] = block[part * 8 : part * 8 + 8]

    outs = iter(outs)

    def take(width, *lists):
        found = {}
        for parts in lists:
            target = next(outs)
            found.update({part: (target, n * width) for n, part in enumerate(parts)})
        return found

    third = take(GROUP, FAR, REST)
    second = take(HALF, (9,), (7, 11), (5, 13), (3, 15), (1,), *[(2 * k,) for k in range(8)])
    first = take(HALF, (8,), (9,), *[(2 * k, 2 * k + 1) for k in NEAR])
    fill(third, 3, 0, GROUP, 0)
    fill(second, 0, 0, GROUP, 0)
    fill(second, 1, 0, GROUP // 2, GROUP)
    fill(first, 1, GROUP // 2, GROUP // 2, 0)
    fill(first, 2, 0, GROUP, GROUP // 2)


def remap(where, targets, trajectory, weights):
    f32 = lambda *shape: jax.ShapeDtypeStruct(shape, jnp.float32)
    smem = pl.BlockSpec(memory_space=pltpu.SMEM)
    vmem = pl.BlockSpec(memory_space=pltpu.VMEM)
    return pl.pallas_call(
        remap_kernel,
        out_shape=[f32(8, 6 * GROUP), f32(8, 10 * GROUP)]
        + [f32(8, n * HALF) for n in (1, 2, 2, 2, 1)]
        + [f32(8, HALF)] * 10
        + [f32(8, 2 * HALF)] * 7,
        in_specs=[smem, smem, pl.BlockSpec(memory_space=pltpu.HBM), vmem],
        out_specs=[vmem] * 24,
        scratch_shapes=[
            pltpu.VMEM((LEV, PTS), jnp.float32),
            pltpu.SemaphoreType.DMA((16,)),
        ]
        + [pltpu.VMEM((CELLS, 128), jnp.float32)] * CHAINS
        + [pltpu.VMEM((BLK, 128), jnp.float32)] * (4 * CHAINS),
        compiler_params=pltpu.CompilerParams(vmem_limit_bytes=48 * 2**20),
    )(where, targets, trajectory, weights)


def fetch_kernel(sources, *refs):
    where_ref, t_ref, w_ref = refs[:3]
    pieces = refs[3 : 3 + len(sources)]
    out_hbm = refs[3 + len(sources)]
    rows, out, out_sem = refs[4 + len(sources) : 7 + len(sources)]
    turned = refs[7 + len(sources) :]
    core, z, y = where_ref[0], where_ref[1], where_ref[2]
    spans = [(part, to, width, piece, source) for piece, given in zip(pieces, sources)
             for part, source, width, to in given]
    for start, group, inside, width in (
        (0, 0, 0, GROUP),
        (GROUP, 1, 0, GROUP // 2),
        (HALF, 1, GROUP // 2, GROUP // 2),
        (HALF + GROUP // 2, 2, 0, GROUP),
        (3 * GROUP, 3, 0, GROUP),
    ):
        base = place(core, group) + inside
        found = {}
        for part, to, length, piece, source in spans:
            if to <= start and start + width <= to + length:
                found[part] = (piece, source + start - to)

        @pl.loop(0, width // 2048)
        def _(i):
            for j in range(16):
                step = i * 2048 + j * 128
                block = jnp.concatenate(
                    [
                        found[part][0][:, pl.ds(pl.multiple_of(found[part][1] + step, 128), 128)]
                        for part in range(16)
                    ],
                    axis=0,
                )
                rows[pl.ds(pl.multiple_of(base + step, 128), 128), :] = block.T

    share = PTS // 4
    stores = []
    for h in range(4):
        for q in range(share // BLK):
            at = h * share + q * BLK
            for u in range(BLK):
                cell = t_ref[at + u]
                turned[q][pl.ds(u, 1), :] = rows[pl.ds(cell, 1), :]
            out[:, pl.ds(at, BLK)] = turned[q][...].T * w_ref[:, pl.ds(at, BLK)]
        for part in range(16):
            store = pltpu.make_async_copy(
                out.at[pl.ds(part * 8, 8), pl.ds(h * share, share)],
                out_hbm.at[pl.ds(level_block(z, y, part), 8), pl.ds(h * share, share)],
                out_sem.at[h * 16 + part],
            )
            store.start()
            stores.append(store)
    for store in stores:
        store.wait()


def fetch(where, cells, weights, pieces, sources):
    smem = pl.BlockSpec(memory_space=pltpu.SMEM)
    vmem = pl.BlockSpec(memory_space=pltpu.VMEM)
    return pl.pallas_call(
        functools.partial(fetch_kernel, sources),
        out_shape=jax.ShapeDtypeStruct((LEV, PTS), jnp.float32),
        in_specs=[smem, smem] + [vmem] * (1 + len(pieces)),
        out_specs=pl.BlockSpec(memory_space=pl.ANY),
        scratch_shapes=[
            pltpu.VMEM((CELLS, 128), jnp.float32),
            pltpu.VMEM((LEV, PTS), jnp.float32),
            pltpu.SemaphoreType.DMA((64,)),
        ]
        + [pltpu.VMEM((BLK, 128), jnp.float32)] * 16,
        compiler_params=pltpu.CompilerParams(vmem_limit_bytes=40 * 2**20),
    )(where, cells, weights, *pieces)


def keep_columns(target, value):
    for c in range(target.shape[0]):
        target[c] = value[:, c * 128 : (c + 1) * 128]


def every(source, start, count, stride):
    return jnp.concatenate(
        [source[c, pl.ds(start, count, stride=stride), :] for c in range(source.shape[0])], axis=1
    )


def forward_kernel(own_ref, p_ref, m_ref, both_ref, y_ref, high_ref, low_ref, o_ref, work):
    b = own_ref[...] + p_ref[...] + m_ref[...]
    a = both_ref[:, :HALF] + y_ref[...]
    rows = [b[:, r * NLON : (r + 1) * NLON] for r in range(12)]
    rows += [a[:, r * NLON : (r + 1) * NLON] for r in range(12)]
    left = halves(jnp.concatenate(rows, axis=0))
    keep_columns(work, split_dot(left, (high_ref[...], low_ref[...])))
    for a in range(8):
        lines = every(work, a, 24, 8)
        for i in range(16):
            o_ref[i, :, a * 32 : (a + 1) * 32] = lines[:, i * 32 : (i + 1) * 32]


def forward(sums, high, low):
    return pl.pallas_call(
        forward_kernel,
        out_shape=jax.ShapeDtypeStruct((16, 24, 256), jnp.float32),
        scratch_shapes=[pltpu.VMEM((4, 192, 128), jnp.float32)],
        compiler_params=pltpu.CompilerParams(vmem_limit_bytes=16 * 2**20),
    )(*sums, high, low)


def legendre_kernel(first_ref, x_ref, high_ref, low_ref, coef_ref, o_ref, lines, back):
    bands = []
    for i in range(16):
        inner, outer = x_ref[i, 0:8], x_ref[i, 8:16]
        if i % 2 == 0:
            if i > 0:
                outer = outer + x_ref[i - 1, 16:24]
            bands += [outer, inner]
        else:
            if i < 15:
                outer = outer + x_ref[i + 1, 16:24]
            bands += [inner, outer]
    keep_columns(lines, jnp.concatenate(bands, axis=0).T)
    coef = jnp.concatenate([coef_ref[...]] * 2, axis=0)
    total = lax.broadcasted_iota(jnp.int32, (16, 256), 1)
    for m in range(16):
        left = jnp.concatenate(
            [every(lines, 2 * m, 8, 32), every(lines, 2 * m + 1, 8, 32)], axis=0
        )
        table = (high_ref[m], low_ref[m])
        spec = split_dot(halves(left), table)
        spec = jnp.where(total >= first_ref[0] + m, spec * coef, 0.0)
        result = split_dot(halves(spec), table, (((1,), (1,)), ((), ())))
        for c in range(2):
            part = result[:, c * 128 : (c + 1) * 128]
            back[c, pl.ds(2 * m, 8, stride=32), :] = part[:8]
            back[c, pl.ds(2 * m + 1, 8, stride=32), :] = part[8:]
    whole = jnp.concatenate([back[c].T for c in range(2)], axis=0)
    nothing = jnp.zeros((8, 256), jnp.float32)
    for i in range(16):
        low, top = whole[16 * i : 16 * i + 8], whole[16 * i + 8 : 16 * i + 16]
        if i % 2 == 0:
            rim = whole[16 * i - 8 : 16 * i] if i > 0 else nothing
            parts = [top, low, rim]
        else:
            rim = whole[16 * i + 16 : 16 * i + 24] if i < 15 else nothing
            parts = [low, top, rim]
        o_ref[i] = jnp.concatenate(parts, axis=0)


def spectral(first, x, table, coef):
    vmem = pl.BlockSpec(memory_space=pltpu.VMEM)
    return pl.pallas_call(
        legendre_kernel,
        out_shape=jax.ShapeDtypeStruct((16, 24, 256), jnp.float32),
        in_specs=[pl.BlockSpec(memory_space=pltpu.SMEM)] + [vmem] * 4,
        scratch_shapes=[pltpu.VMEM((2, 256, 128), jnp.float32)] * 2,
        compiler_params=pltpu.CompilerParams(vmem_limit_bytes=24 * 2**20),
    )(first, x, *table, coef)


def split_kernel(x_ref, high_ref, low_ref):
    @pl.loop(0, x_ref.shape[0])
    def _(m):
        high_ref[m], low_ref[m] = halves(x_ref[m])


def split_table(x):
    half = jax.ShapeDtypeStruct(x.shape, jnp.bfloat16)
    return pl.pallas_call(
        split_kernel,
        out_shape=[half, half],
        cost_estimate=pl.CostEstimate(
            flops=4 * x.size, bytes_accessed=8 * x.size, transcendentals=0
        ),
        compiler_params=pltpu.CompilerParams(vmem_limit_bytes=24 * 2**20),
    )(x)


def inverse_kernel(x_ref, high_ref, low_ref, a_ref, b_ref, work, lines):
    for a in range(8):
        for i in range(16):
            work[a * 24 : (a + 1) * 24, i * 32 : (i + 1) * 32] = x_ref[i, :, a * 32 : (a + 1) * 32]
    table = (high_ref[...], low_ref[...])
    keep_columns(lines, split_dot(halves(work[...]), table, (((1,), (1,)), ((), ()))))
    for r in range(24):
        out = a_ref if r < 12 else b_ref
        at = (r % 12) * NLON
        out[:, at : at + NLON] = every(lines, r, 8, 24)


def inverse(x, high, low):
    half = jax.ShapeDtypeStruct((8, HALF), jnp.float32)
    return pl.pallas_call(
        inverse_kernel,
        out_shape=[half, half],
        scratch_shapes=[pltpu.VMEM((192, 512), jnp.float32), pltpu.VMEM((4, 192, 128), jnp.float32)],
        compiler_params=pltpu.CompilerParams(vmem_limit_bytes=16 * 2**20),
    )(x, high, low)


ALONG = [(b, (b + 2) % 16) for b in range(16)]
AGAINST = [(b, (b - 2) % 16) for b in range(16)]
ACROSS = [(b, b ^ 1) for b in range(16)]


def ahead(x):
    return lax.ppermute(x, "bulk", ALONG)


def behind(x):
    return lax.ppermute(x, "bulk", AGAINST)


def across(x):
    return lax.ppermute(x, "bulk", ACROSS)


def other_core(x):
    return lax.ppermute(x, "inner", ACROSS)


def loosely(*moves, free=(), late=()):
    results = [move(value) for move, value in list(moves) + list(free)]
    held = lax.optimization_barrier(tuple(results[: len(moves)]) + tuple(late))
    return held[: len(moves)], results[len(moves) :], held[len(moves) :]


def together(*moves, free=(), late=()):
    both = list(moves) + list(free)
    values = lax.optimization_barrier(tuple(value for _, value in both))
    both = [(move, value) for (move, _), value in zip(both, values)]
    return loosely(*both[: len(moves)], free=both[len(moves) :], late=late)


def wide(*blocks):
    return jnp.concatenate(blocks, axis=1)


def gather_sums(legendre, targets, cross_far, cross, y1, y2, y3, y4, y5, *rest):
    keep, far_p, far_m = rest[:8], rest[8], rest[9]
    flat = lambda k: rest[10 + NEAR.index(k)]
    quarter = HALF // 2

    def with_core(piece, add):
        return wide(piece[:, :GROUP] + add, piece[:, GROUP:])

    def part_of(source, n, width):
        return source[:, n * width : (n + 1) * width]

    (shared_far,), (p, m), _ = loosely(
        (other_core, cross_far), free=[(ahead, far_p), (behind, far_m)]
    )

    def from_core(k, r):
        source, parts = (shared_far, FAR) if k in (3, 4, 5) else (shared, REST)
        return part_of(source, parts.index(2 * k + r), GROUP)

    mine = lambda k: with_core(keep[k], from_core(k, 0))
    send = lambda piece, *order: wide(
        *[with_core(part_of(piece, i, HALF), from_core(k, 1)) for i, k in enumerate(order)]
    )
    (y, shared), _, (p, m) = loosely(
        (across, send(y1, 4)), (other_core, cross), late=[p, m]
    )
    here = mine(4) + y
    at_home = with_core(y5, from_core(0, 1))
    (p, y), (m,), _ = loosely(
        (ahead, wide(flat(3) + wide(p, jnp.zeros_like(p)), here[:, :quarter])),
        (across, wide(send(y2, 3, 5), at_home[:, :quarter])),
        free=[(behind, wide(flat(5) + wide(jnp.zeros_like(m), m), here[:, quarter:]))],
    )
    here_p = mine(3) + y[:, :HALF]
    here_m = mine(5) + y[:, HALF : 2 * HALF]
    here_p = wide(here_p[:, :quarter] + p[:, 2 * HALF :], here_p[:, quarter:])
    here_m = wide(here_m[:, :quarter], here_m[:, quarter:] + m[:, 2 * HALF :])
    home = y[:, 2 * HALF :]
    held_targets, y = lax.optimization_barrier((targets, y))
    (p, y, cells), (m,), _ = loosely(
        (ahead, wide(flat(2) + p[:, : 2 * HALF], here_p)),
        (across, wide(send(y3, 2, 6), at_home[:, quarter:])),
        (lambda t: t & (CELLS - 1), held_targets),
        free=[(behind, wide(flat(6) + m[:, : 2 * HALF], here_m))],
    )
    own = mine(0) + wide(home, y[:, 2 * HALF :])
    (p, y), (m,), _ = loosely(
        (ahead, wide(flat(1), mine(2) + y[:, :HALF]) + p),
        (across, send(y4, 1, 7)),
        free=[(behind, wide(flat(7), mine(6) + y[:, HALF : 2 * HALF]) + m)],
    )
    both = flat(0) + p[:, : 2 * HALF] + m[:, : 2 * HALF]
    p, m, y, table = loosely(
        (ahead, mine(1) + y[:, :HALF] + p[:, 2 * HALF :]),
        (behind, mine(7) + y[:, HALF:] + m[:, 2 * HALF :]),
        (across, both[:, HALF:]),
        (split_table, legendre),
    )[0]
    return (own, p, m, both, y), table, cells


def spread_field(a, b):
    pieces, sources = [], []
    quarter = HALF // 2

    def give(piece, *spans):
        pieces.append(piece)
        sources.append(spans)

    def first(k, r, source):
        return (2 * k + r, source, HALF, 0)

    def second(k, r, source):
        return (2 * k + r, source, HALF, HALF)

    def all_of(k, source):
        return [second(k, 0, source), second(k, 1, source + HALF)]

    def heads(*given):
        value = wide(*[array[:, at : at + GROUP] for _, array, at in given])
        return value, [(part, n * GROUP, GROUP, 3 * GROUP) for n, (part, _, _) in enumerate(given)]

    give(a, first(0, 0, 0))
    give(b, second(0, 0, 0))
    (p1, m1, y0), _, _ = together((ahead, a), (behind, a), (across, b))
    give(y0, second(0, 1, 0))
    give(p1, first(7, 0, 0))
    give(m1, first(1, 0, 0))
    pair = wide(b, y0)
    (p, m), (y1,), _ = together(
        (ahead, wide(pair, p1)),
        (behind, wide(pair, m1)),
        free=[(across, wide(a, p1, m1))],
    )
    give(p, *all_of(7, 0), first(6, 0, 2 * HALF))
    give(m, *all_of(1, 0), first(2, 0, 2 * HALF))
    core1, spans1 = heads(
        (0, a, 0), (14, p1, 0), (2, m1, 0), (12, p, 2 * HALF), (4, m, 2 * HALF)
    )
    (p, m, y2), (core1,), (y1,) = together(
        (ahead, p),
        (behind, m),
        (across, wide(p[:, 2 * HALF :], m[:, 2 * HALF :])),
        free=[(other_core, core1)],
        late=[y1],
    )
    give(y1, first(0, 1, 0), first(7, 1, HALF), first(1, 1, 2 * HALF))
    give(p, *all_of(6, 0), first(5, 0, 2 * HALF))
    give(m, *all_of(2, 0), first(3, 0, 2 * HALF))
    core2, spans2 = heads(
        (1, y1, 0), (15, y1, HALF), (3, y1, 2 * HALF), (10, p, 2 * HALF), (6, m, 2 * HALF)
    )
    (p, m, y3), (core2,), (core1,) = together(
        (ahead, p[:, : 2 * HALF + quarter]),
        (behind, wide(m[:, : 2 * HALF], m[:, 2 * HALF + quarter :])),
        (across, wide(p[:, 2 * HALF :], m[:, 2 * HALF :])),
        free=[(other_core, core2)],
        late=[core1],
    )
    give(core1, *spans1)
    give(y2, first(6, 1, 0), first(2, 1, HALF))
    give(p, *all_of(5, 0))
    give(m, *all_of(3, 0))
    far = wide(p[:, 2 * HALF :], m[:, 2 * HALF :])
    give(far, first(4, 0, 0))
    core3, spans3 = heads((13, y2, 0), (5, y2, HALF), (8, far, 0))
    (p, m, y4), (core3,), (core2,) = together(
        (ahead, p[:, :HALF]),
        (behind, m[:, HALF : 2 * HALF]),
        (across, far),
        free=[(other_core, core3)],
        late=[core2],
    )
    give(core2, *spans2)
    give(y3, first(5, 1, 0), first(3, 1, HALF))
    give(p, second(4, 0, 0))
    give(m, second(4, 1, 0))
    give(y4, first(4, 1, 0))
    core4, spans4 = heads((11, y3, 0), (7, y3, HALF), (9, y4, 0))
    (core4,), _, (core3,) = together((other_core, core4), late=[core3])
    give(core3, *spans3)
    give(core4, *spans4)
    return pieces, sources


def shards(trajectory, targets, remap_weights, legendre, spectral_coef):
    inner = lax.axis_index("inner")
    bulk = lax.axis_index("bulk")
    where = jnp.stack([inner % 2, bulk // 2, bulk % 2]).astype(jnp.int32)
    weights = remap_weights[None, :]
    high, low = (jnp.asarray(t) for t in tables())
    sums, table, cells = gather_sums(legendre, targets, *remap(where, targets, trajectory, weights))
    sent = lax.all_to_all(forward(sums, high, low), "inner", 0, 0, tiled=True)
    first = (inner * 16).astype(jnp.int32)[None]
    back = spectral(first, sent, table, spectral_coef)
    back = lax.all_to_all(back, "inner", 0, 0, tiled=True)
    pieces, sources = spread_field(*inverse(back, high, low))
    return fetch(where, cells, weights, pieces, sources)


def solution(mesh):
    placed = (
        P(None, ("inner", "bulk")),
        P(("inner", "bulk")),
        P(("inner", "bulk")),
        P("inner", None, None),
        P("bulk", None),
    )
    return jax.shard_map(
        shards, mesh=mesh, in_specs=placed, out_specs=P(None, ("inner", "bulk")), check_vma=False
    )
```
